32 devices in a mesh: section: 2 (over core), dp: 4 (over z), mp: 4 (over y, x).
Axes of the slice: x: 2, y: 2, z: 4, core: 2. Of those that a mesh axis runs over, the one named last changes fastest.
Arguments:
- fwd_in: bfloat16 [2, 4, 4, 256, 3072], P('section', 'dp', 'mp'), may hold values from -6 to 6
- kept_in: bfloat16 [2, 4, 4, 256, 3072], P('section', 'dp', 'mp'), may hold values from -6 to 6
- cotangent: bfloat16 [2, 4, 4, 256, 3072], P('section', 'dp', 'mp'), may hold values from -6 to 6
- weight: bfloat16 [2, 12288, 12288], P('section', 'mp', 'dp'), may hold values from -1 to 1
- bias: float32 [2, 12288], P('section', 'dp'), may hold values from -3 to 3
- norm_gain: float32 [2, 12288], P('section', 'mp'), may hold values from 0.1 to 1.9
- norm_shift: float32 [2, 12288], P('section', 'mp'), may hold values from -3 to 3
Outputs:
- next_in: bfloat16 [2, 4, 4, 256, 3072], P('section', 'dp', 'mp')
- passed: bfloat16 [2, 4, 4, 256, 3072], P('section', 'dp', 'mp')
- weight_grad: float32 [2, 12288, 12288], P('section', 'mp', 'dp')
- bias_grad: float32 [2, 12288], P('section', 'dp')
- norm_grads: float32 [2, 2, 12288], P('section', None, 'mp')
The draws below stay inside these ranges and needn't reach their ends.
All inputs are finite; a program needn't handle non-finite values.
Results may differ from the reference program's by a relative error of at most 0.018.
Values may be sent and summed in bfloat16 or wider, within the bound.
No kernel may reach another device: no remote copies, remote signals or barrier semaphores. Data moves between devices by JAX's collectives and lax.ppermute only.
A program may use at most 128 MiB of HBM per device.

```python
import jax
import jax.numpy as jnp
from jax import lax

D = 12288
POS = 256
TOKENS = 1024
N_DP = 4
N_MP = 4


def tilted_matrix(key, noise, low_end, high_end):
    sign_key, rough_key = jax.random.split(key)
    signs = jnp.where(jax.random.bernoulli(sign_key, 0.5, (2, 1, D)), 1.0, -1.0).astype(jnp.float32)
    place = jnp.arange(D, dtype=jnp.float32) / (D - 1)
    rising = jnp.exp(jnp.log(low_end) + (jnp.log(high_end) - jnp.log(low_end)) * place)
    rough = jax.random.uniform(rough_key, (2, D, D), jnp.float32, 0.6, 1.4)
    common = 0.15 * signs * rising[None, :, None] * rough
    return ((noise + common) * D ** (-0.5)).astype(jnp.bfloat16)


def draw_weight(key, part):
    key = jax.random.fold_in(key, 11)
    noise_key, tilt_key = jax.random.split(key)
    noise = jnp.clip(jax.random.normal(noise_key, (2, D, D), jnp.float32), -6.0, 6.0)
    return tilted_matrix(tilt_key, noise, 0.3, 3.0)


def steps_of(key, shape, cuts, smallest, top_value):
    loudness, own = 1.0, jax.random.fold_in(key, 6)
    for axis_at, parts in cuts:
        steps = jnp.exp(jax.random.uniform(jax.random.fold_in(own, axis_at), (parts,), jnp.float32, smallest / len(cuts), top_value / len(cuts)))
        loudness = loudness * jnp.repeat(steps, shape[axis_at] // parts).reshape([-1 if axis == axis_at else 1 for axis in range(len(shape))])
    return loudness


def centred(rng, dims, scale, most, shards=(), kind=jnp.bfloat16):
    gain = steps_of(rng, dims, shards, -0.22, 0.18) if shards else 1.0
    result = jax.random.normal(rng, dims, jnp.float32) * scale * gain
    return jnp.minimum(jnp.maximum(result, -most), most).astype(kind)


def setup_inputs(seed: int = 0) -> dict:
    key_list = jax.random.split(jax.random.key(seed), 8)
    fwd_in = centred(key_list[0], (2, N_DP, N_MP, POS, D // N_MP), 1.0, 6.0, ((0, 2), (1, 4), (2, 4)))
    kept_in = centred(key_list[1], (2, N_DP, N_MP, POS, D // N_MP), 1.0, 6.0, ((0, 2), (1, 4), (2, 4)))
    cotangent = centred(key_list[2], (2, N_DP, N_MP, POS, D // N_MP), 1.0, 6.0, ((0, 2), (1, 4), (2, 4)))
    weight = draw_weight(jax.random.fold_in(key_list[7], 71), 0)
    bias = centred(key_list[4], (2, D), 0.5, 3.0, ((0, 2), (1, 4)), jnp.float32)
    norm_gain = jnp.clip(1.0 + 0.18 * jax.random.normal(key_list[5], (2, D), jnp.float32), 0.1, 1.9)
    norm_shift = centred(key_list[6], (2, D), 0.5, 3.0, ((0, 2), (1, 4)), jnp.float32)
    return dict(fwd_in=fwd_in, kept_in=kept_in, cotangent=cotangent, weight=weight, bias=bias, norm_gain=norm_gain, norm_shift=norm_shift)


eps = 1e-05

def from_in(blocks):
    return blocks.transpose(0, 2, 1, 3).reshape(TOKENS, D)

def from_out(blocks):
    return blocks.transpose(1, 2, 0, 3).reshape(TOKENS, D)

def to_in(matrix):
    return matrix.reshape(N_DP, POS, N_MP, D // N_MP).transpose(0, 2, 1, 3)

def to_out(matrix):
    return matrix.reshape(N_MP, POS, N_DP, D // N_MP).transpose(2, 0, 1, 3)

def relabel(matrix):
    shaped = matrix.reshape(N_DP, N_DP, POS // N_DP, N_MP, N_MP, D // (N_MP * N_MP))
    return shaped.transpose(1, 0, 2, 4, 3, 5).reshape(TOKENS, D)

def normalize(values, gain_row, shift_row):
    floats = values.astype(jnp.float32)
    mean_val = lax.optimization_barrier(jnp.mean(floats, 1, keepdims=True))
    spread = lax.optimization_barrier(jnp.mean(floats * floats, 1, keepdims=True)) - mean_val * mean_val
    inverse = lax.rsqrt(spread + eps)
    normal = (floats - mean_val) * inverse
    return (normal, inverse, (normal * gain_row + shift_row).astype(jnp.bfloat16))

def rounded(values):
    return lax.optimization_barrier(values.astype(jnp.bfloat16)).astype(jnp.float32)

def section_pass(fresh_rows, kept_rows, upstream, weight_full, bias_row, gain_row, shift_row):
    block_width = D // N_MP
    normal_x, inverse_x, normed = normalize(fresh_rows, gain_row, shift_row)
    normal_k, inverse_k, normed_kept = normalize(kept_rows, gain_row, shift_row)
    summed = jnp.zeros((TOKENS, D), jnp.float32)
    for block in range(N_MP):
        low = block * block_width
        term = jnp.dot(normed[:, low:low + block_width], weight_full[low:low + block_width], preferred_element_type=jnp.float32)
        summed = summed + rounded(term)
    output = (summed + bias_row[None, :]).astype(jnp.bfloat16)
    weight_grad = lax.dot_general(normed_kept, upstream, (((0,), (0,)), ((), ())), preferred_element_type=jnp.float32)
    bias_grad = lax.optimization_barrier(jnp.sum(upstream.astype(jnp.float32), 0))
    grad_rows = jnp.zeros((TOKENS, D), jnp.float32)
    for block in range(N_DP):
        low = block * block_width
        term = lax.dot_general(upstream[:, low:low + block_width], weight_full[:, low:low + block_width], (((1,), (1,)), ((), ())), preferred_element_type=jnp.float32)
        grad_rows = grad_rows + rounded(term)
    gain_grad = lax.optimization_barrier(jnp.sum(grad_rows * normal_k, 0))
    shift_grad = lax.optimization_barrier(jnp.sum(grad_rows, 0))
    scaled = grad_rows * gain_row[None, :]
    first_mean = lax.optimization_barrier(jnp.mean(scaled, 1, keepdims=True))
    second_mean = lax.optimization_barrier(jnp.mean(scaled * normal_k, 1, keepdims=True))
    input_grad = (inverse_k * (scaled - first_mean - normal_k * second_mean)).astype(jnp.bfloat16)
    return (output, input_grad, weight_grad, bias_grad, jnp.stack([gain_grad, shift_grad]))

def reference(fwd_in, kept_in, cotangent, weight, bias, norm_gain, norm_shift):
    results = []
    for section_slot in range(2):
        results.append(section_pass(from_in(fwd_in[section_slot]), from_in(kept_in[section_slot]), from_out(cotangent[section_slot]), weight[section_slot], bias[section_slot].astype(jnp.float32), norm_gain[section_slot].astype(jnp.float32), norm_shift[section_slot].astype(jnp.float32)))
    first, second = (results[0], results[1])
    next_in = jnp.stack([to_out(relabel(second[1])), to_in(relabel(first[0]))])
    passed = jnp.stack([to_in(first[1]), to_out(second[0])])
    weight_grad = jnp.stack([first[2], second[2]])
    bias_grad = jnp.stack([first[3], second[3]])
    norm_grads = jnp.stack([first[4], second[4]])
    return (next_in, passed, weight_grad, bias_grad, norm_grads)
```

```python
import functools

import jax
import jax.numpy as jnp
from jax import lax
from jax.experimental import pallas as pl
from jax.experimental.pallas import tpu as pltpu
from jax.sharding import PartitionSpec as P

eps = 1e-05
V_CHUNKS = 4
LIGHT = pl.CostEstimate(flops=1, bytes_accessed=1, transcendentals=0)


def after(value, *others):
    return lax.optimization_barrier((value,) + others)[0]


def ring_total(value, axis):
    n = lax.axis_size(axis)
    parts = [
        lax.ppermute(value, axis, [(s, (s + k) % n) for s in range(n)]) for k in range(1, n)
    ]
    total = value
    for part in parts:
        total = total + part
    return total


def flip(value, axis, mask):
    n = lax.axis_size(axis)
    return lax.ppermute(value, axis, [(s, s ^ mask) for s in range(n)])


def pieces_of(matrix, groups, swapped):
    rows, cols = matrix.shape[0] // groups, matrix.shape[1] // groups
    cut = lambda r, c: matrix[r * rows:(r + 1) * rows, c * cols:(c + 1) * cols]
    pairs = [(a, b) for a in range(groups) for b in range(groups)]
    return jnp.stack([cut(b, a) if swapped else cut(a, b) for a, b in pairs])


def matrix_of(pieces, groups, swapped):
    at = lambda r, c: pieces[c * groups + r] if swapped else pieces[r * groups + c]
    return jnp.concatenate(
        [jnp.concatenate([at(r, c) for c in range(groups)], 1) for r in range(groups)], 0
    )


def grad_kernel(v_ref, c_ref, *rest):
    out_ref, turned = rest[-2:]

    @pl.when(pl.program_id(0) == 0)
    def _():
        turned[...] = v_ref[...].T

    out_ref[...] = jnp.dot(turned[...], c_ref[...], preferred_element_type=jnp.float32)


def grad_block(kept_block, upstream, filled, block, blocks):
    tokens, width = kept_block.shape
    cols = upstream.shape[1]
    step = 768
    specs = [
        pl.BlockSpec((tokens, width), lambda j: (0, 0)),
        pl.BlockSpec((tokens, step), lambda j: (0, j)),
    ]
    operands = [kept_block, upstream]
    aliases = {}
    if filled is not None:
        specs.append(pl.BlockSpec(memory_space=pl.ANY))
        operands.append(filled)
        aliases = {2: 0}
    return pl.pallas_call(
        grad_kernel,
        grid=(cols // step,),
        in_specs=specs,
        out_specs=pl.BlockSpec((width, step), lambda j: (block, j)),
        out_shape=jax.ShapeDtypeStruct((width * blocks, cols), jnp.float32),
        scratch_shapes=[pltpu.VMEM((width, tokens), jnp.bfloat16)],
        input_output_aliases=aliases,
        compiler_params=pltpu.CompilerParams(vmem_limit_bytes=32 * 2**20),
        cost_estimate=LIGHT,
    )(*operands)


def share_kernel(count, turned, *refs):
    w_ref, out_ref = refs[count], refs[-1]
    dims = (((1,), (1 if turned else 0,)), ((), ()))
    for k in range(count):
        out_ref[k] = lax.dot_general(
            refs[k][...], w_ref[...], dims, preferred_element_type=jnp.float32
        ).astype(jnp.bfloat16)


def shares(blocks, w, turned, filled, at, total):
    count = len(blocks)
    rows, depth = blocks[0].shape
    cols = w.shape[0] if turned else w.shape[1]
    step = 512
    specs = [pl.BlockSpec((rows, depth), lambda j: (0, 0))] * count
    if turned:
        specs.append(pl.BlockSpec((step, depth), lambda j: (j, 0)))
    else:
        specs.append(pl.BlockSpec((depth, step), lambda j: (0, j)))
    operands = list(blocks) + [w]
    aliases = {}
    if filled is not None:
        specs.append(pl.BlockSpec(memory_space=pl.ANY))
        operands.append(filled)
        aliases = {count + 1: 0}
    return pl.pallas_call(
        functools.partial(share_kernel, count, turned),
        grid=(cols // step,),
        in_specs=specs,
        out_specs=pl.BlockSpec((count, rows, step), lambda j: (at // count, 0, j)),
        out_shape=jax.ShapeDtypeStruct((total, rows, cols), jnp.bfloat16),
        input_output_aliases=aliases,
        compiler_params=pltpu.CompilerParams(vmem_limit_bytes=32 * 2**20),
        cost_estimate=LIGHT,
    )(*operands)


def boundary_kernel(g_ref, kept_ref, columns_ref, gain_ref, h_ref, h1_ref, h2_ref, bias_ref, section_ref, passed_ref, out_ref):
    step = pl.program_id(0)
    first = section_ref[0] == 0
    groups = pl.num_programs(0)
    width = out_ref.shape[2]
    f32 = jnp.float32
    columns = columns_ref[...]
    mean, inverse, one, two = (columns[:, k:k + 1] for k in range(4))
    for f in range(out_ref.shape[0] // 4):
        cut = pl.ds(f * width, width)
        hat = (kept_ref[:, cut].astype(f32) - mean) * inverse
        grad = (inverse * (g_ref[:, cut] * gain_ref[:, cut] - one - hat * two)).astype(jnp.bfloat16)
        summed = h_ref[:, cut].astype(f32) + h1_ref[:, cut].astype(f32) + h2_ref[:, cut].astype(f32)
        output = (summed + bias_ref[:, cut]).astype(jnp.bfloat16)
        passed_ref[:, cut] = jnp.where(first, grad, output)
        out_ref[jnp.where(first, step * groups + f, f * groups + step)] = jnp.where(
            first, output, grad
        )


def boundary(grad_rows, kept_rows, columns, gain, h0, h1, h2, bias, section):
    rows, cols = grad_rows.shape
    part = rows // 4
    wide = pl.BlockSpec((part, cols), lambda j: (j, 0))
    line = pl.BlockSpec((1, cols), lambda j: (0, 0))
    return pl.pallas_call(
        boundary_kernel,
        grid=(4,),
        in_specs=[
            wide, wide, pl.BlockSpec((part, 4), lambda j: (j, 0)), line, wide, wide, wide, line,
            pl.BlockSpec(memory_space=pltpu.SMEM),
        ],
        out_specs=[wide, pl.BlockSpec((16, part, cols // 4), lambda j: (0, 0, 0))],
        out_shape=[
            jax.ShapeDtypeStruct((rows, cols), jnp.bfloat16),
            jax.ShapeDtypeStruct((16, part, cols // 4), jnp.bfloat16),
        ],
        compiler_params=pltpu.CompilerParams(vmem_limit_bytes=32 * 2**20),
        cost_estimate=LIGHT,
    )(
        grad_rows, kept_rows, columns, gain.reshape(1, cols), h0, h1, h2, bias.reshape(1, cols),
        section.reshape(1),
    )


def from_partner(value, axis, stride):
    mask = 2**stride
    pairs = [(source, source ^ mask) for source in range(lax.axis_size(axis))]
    return lax.ppermute(value, axis, pairs)


def standardize(values, totals, squares, full_width):
    mean_val = totals / full_width
    spread = squares / full_width - mean_val * mean_val
    inv_std = lax.rsqrt(spread + eps)
    return ((values - mean_val[:, None]) * inv_std[:, None], inv_std)


def regroup(outgoing, groups):
    flat_buffer = outgoing.reshape((groups * groups,) + outgoing.shape[2:])
    moved_data = lax.all_to_all(flat_buffer, ("dp", "mp"), split_axis=0, concat_axis=0, tiled=True)
    return moved_data.reshape(outgoing.shape)


def shards_of_any_size(fwd_in, kept_in, cotangent, weight, bias, norm_gain, norm_shift):
    section_index = lax.axis_index("section")
    groups = lax.axis_size("dp")
    row_count = fwd_in.shape[3]
    col_count = fwd_in.shape[4]
    full_width = col_count * lax.axis_size("mp")
    piece_rows = row_count // groups
    piece_cols = col_count // groups
    weight_tile = weight.reshape(col_count, col_count)
    gain_cols = norm_gain.reshape(col_count)
    shift_cols = norm_shift.reshape(col_count)
    fresh_rows = fwd_in.reshape(row_count, col_count).astype(jnp.float32)
    kept_values = kept_in.reshape(row_count, col_count).astype(jnp.float32)
    upstream = cotangent.reshape(row_count, col_count)
    row_stats = lax.psum(
        (
            jnp.sum(fresh_rows, 1),
            jnp.sum(fresh_rows * fresh_rows, 1),
            jnp.sum(kept_values, 1),
            jnp.sum(kept_values * kept_values, 1),
        ),
        "mp",
    )
    fresh_hat, unused_scale = standardize(fresh_rows, row_stats[0], row_stats[1], full_width)
    kept_hat, kept_inv = standardize(kept_values, row_stats[2], row_stats[3], full_width)
    normed = (fresh_hat * gain_cols + shift_cols).astype(jnp.bfloat16)
    normed_kept = (kept_hat * gain_cols + shift_cols).astype(jnp.bfloat16)
    upstream_all = lax.all_gather(upstream, "mp", axis=0, tiled=True)
    gathered, gathered_kept = (
        lax.all_gather(normed, "dp", axis=0, tiled=True),
        lax.all_gather(normed_kept, "dp", axis=0, tiled=True),
    )
    weight_grad = lax.dot_general(
        gathered_kept, upstream_all, (((0,), (0,)), ((), ())), preferred_element_type=jnp.float32
    )
    segment = gathered
    summed = lax.psum_scatter(
        jnp.dot(segment, weight_tile, preferred_element_type=jnp.float32).astype(jnp.bfloat16),
        "mp",
        scatter_dimension=0,
        tiled=True,
    ).astype(jnp.float32)
    output = (summed + bias.reshape(col_count)).astype(jnp.bfloat16)
    bias_grad = jnp.sum(upstream_all, 0, dtype=jnp.float32)
    segment = upstream_all
    grad_rows = lax.psum_scatter(
        lax.dot_general(
            segment, weight_tile, (((1,), (1,)), ((), ())), preferred_element_type=jnp.float32
        ).astype(jnp.bfloat16),
        "dp",
        scatter_dimension=0,
        tiled=True,
    ).astype(jnp.float32)
    scaled = grad_rows * gain_cols
    column_grads = lax.psum((jnp.sum(grad_rows * kept_hat, 0), jnp.sum(grad_rows, 0)), "dp")
    row_terms = lax.psum((jnp.sum(scaled, 1), jnp.sum(scaled * kept_hat, 1)), "mp")
    input_grad = (
        kept_inv[:, None]
        * (
            scaled
            - row_terms[0][:, None] / full_width
            - kept_hat * (row_terms[1][:, None] / full_width)
        )
    ).astype(jnp.bfloat16)
    out_pack = output.reshape(groups, piece_rows, groups, piece_cols).transpose(0, 2, 1, 3)
    grad_pack = input_grad.reshape(groups, piece_rows, groups, piece_cols).transpose(2, 0, 1, 3)
    outgoing = jnp.where(section_index == 0, out_pack, grad_pack)
    arrived = from_partner(regroup(outgoing, groups), "section", 0)
    as_cotangent = arrived.transpose(0, 2, 1, 3).reshape(row_count, col_count)
    as_input = arrived.transpose(1, 2, 0, 3).reshape(row_count, col_count)
    next_in = jnp.where(section_index == 0, as_cotangent, as_input)
    passed = jnp.where(section_index == 0, input_grad, output)
    return (
        next_in.reshape(fwd_in.shape),
        passed.reshape(fwd_in.shape),
        weight_grad.reshape(1, col_count, col_count),
        bias_grad.reshape(1, col_count),
        jnp.stack([column_grads[0], column_grads[1]]).reshape(1, 2, col_count),
    )


PAIRS = [(0, 1), (1, 0), (2, 3), (3, 2)]
MIDDLE = [(1, 2), (2, 1)]
INWARD = [(0, 1), (3, 2)]
OUTWARD = [(1, 0), (2, 3)]


def shards_of_four(fwd_in, kept_in, cotangent, weight, bias, norm_gain, norm_shift):
    f32, bf16 = jnp.float32, jnp.bfloat16
    section = lax.axis_index("section")
    dp, mp = lax.axis_index("dp"), lax.axis_index("mp")
    inner = (dp == 1) | (dp == 2)
    row_count, col_count = fwd_in.shape[3], fwd_in.shape[4]
    full_width = col_count * 4
    half = col_count // 2
    w = weight.reshape(weight.shape[1], weight.shape[2])
    gain = norm_gain.reshape(col_count)
    shift = norm_shift.reshape(col_count)
    fresh_rows = fwd_in.reshape(row_count, col_count)
    kept_rows = kept_in.reshape(row_count, col_count)
    upstream = cotangent.reshape(row_count, col_count)
    along = lambda value, pairs: lax.ppermute(value, "dp", pairs)
    pick = lambda stack, k: lax.dynamic_index_in_dim(stack, k, 0, keepdims=False)

    def standardize(values, mean, square_mean):
        inverse = lax.rsqrt(square_mean - mean * mean + eps)
        return (values.astype(f32) - mean[:, None]) * inverse[:, None], inverse

    def affine(hat):
        return (hat * gain + shift).astype(bf16)

    def added(one, two):
        return (one.astype(f32) + two.astype(f32)).astype(bf16)

    u1a, u1b = along(fresh_rows, PAIRS), along(fresh_rows, MIDDLE)
    c1, c2 = flip(upstream, "mp", 1), flip(upstream, "mp", 2)
    fresh, kept = fresh_rows.astype(f32), kept_rows.astype(f32)
    sums = jnp.stack(
        [jnp.sum(fresh, 1), jnp.sum(fresh * fresh, 1), jnp.sum(kept, 1), jnp.sum(kept * kept, 1)]
    )
    sums = sums + flip(sums, "mp", 1)
    stats = (sums + flip(sums, "mp", 2)) / full_width
    g_stack = shares([upstream], w, True, None, 2, 4)
    u1a, u1b, c1, c2, stats, g_stack = lax.optimization_barrier(
        (u1a, u1b, c1, c2, stats, g_stack)
    )

    u2in, u2out = along(u1a, MIDDLE), along(u1b, OUTWARD)
    c3l, c3r = flip(c1[:, :half], "mp", 2), flip(c2[:, half:], "mp", 1)
    kept_hat, kept_inv = standardize(kept_rows, stats[2], stats[3])
    normed_kept = affine(kept_hat)
    far1 = along(normed_kept, INWARD)
    g_stack = shares([c1, c2], w, True, g_stack, 0, 4)
    all_stats = lax.all_gather(stats[:2], "dp", axis=0)
    c3 = jnp.concatenate([c3l, c3r], 1)
    g_stack = shares([c3], w, True, g_stack, 3, 4)
    u2in, u2out, far1, g_stack = lax.optimization_barrier((u2in, u2out, far1, g_stack))

    def g_block(k):
        apart = lax.bitwise_xor(lax.bitwise_xor(dp, mp), k)
        return pick(g_stack, jnp.where(apart == 0, 2, jnp.where(apart == 3, 3, apart - 1)))

    u3 = along(u2in, OUTWARD)
    r1 = along(g_block(3), INWARD)
    far2 = along(far1, MIDDLE)

    def normed(rows, block):
        row_stats = pick(all_stats, block)
        hat, unused = standardize(rows, row_stats[0], row_stats[1])
        return affine(hat)

    n0 = normed(fresh_rows, dp)
    n1 = normed(u1a, lax.bitwise_xor(dp, 1))
    n2 = normed(jnp.where(inner, u1b, u2out), jnp.where(inner, dp ^ 3, dp ^ 2))
    h_stack = shares([n0, n1, n2], w, False, None, 0, 4)
    u3, r1, far2, h_stack = lax.optimization_barrier((u3, r1, far2, h_stack))

    x2 = added(g_block(2), r1)
    r2out, r2in = along(x2, INWARD), along(x2, MIDDLE)
    far3 = along(far2, OUTWARD)
    n3 = normed(jnp.where(inner, u2in, u3), jnp.where(inner, dp ^ 2, dp ^ 3))
    h_stack = shares([n3], w, False, h_stack, 3, 4)

    def h_block(k):
        apart = lax.bitwise_xor(lax.bitwise_xor(dp, mp), k)
        return pick(h_stack, jnp.where(inner & (apart >= 2), apart ^ 1, apart))

    h_far = h_block(3)
    left, right = flip(h_far[:, :half], "mp", 1), flip(h_far[:, half:], "mp", 2)
    r2out, r2in, far3, h_stack = lax.optimization_barrier((r2out, r2in, far3, h_stack))

    r3a = along(added(g_block(1), r2in), PAIRS)
    r3b = along(added(g_block(3), r2out), MIDDLE)
    h_two, h_one = h_block(2), h_block(1)
    h_two = jnp.concatenate([added(h_two[:, :half], left), h_two[:, half:]], 1)
    h_one = jnp.concatenate([h_one[:, :half], added(h_one[:, half:], right)], 1)
    h_from_one, h_from_two = flip(h_one, "mp", 1), flip(h_two, "mp", 2)
    c_stack = jnp.stack([upstream, c1, c2, c3])
    block_sums = jnp.sum(c_stack, 1, dtype=f32)
    in_order = [pick(block_sums, lax.bitwise_xor(mp, b)) for b in range(4)]
    bias_grad = in_order[0] + in_order[1] + in_order[2] + in_order[3]
    c_of = lambda k: pick(c_stack, lax.bitwise_xor(lax.bitwise_xor(dp, mp), k))
    c_all = jnp.concatenate(
        [c_of(0), c_of(1), c_of(jnp.where(inner, 3, 2)), c_of(jnp.where(inner, 2, 3))]
    )
    r3a, r3b, h_from_one, h_from_two, c_all, normed_kept = lax.optimization_barrier(
        (r3a, r3b, h_from_one, h_from_two, c_all, normed_kept)
    )

    near1, near2 = along(normed_kept, MIDDLE), along(normed_kept, OUTWARD)
    grad_rows = g_block(0).astype(f32) + r3a.astype(f32) + r3b.astype(f32)
    scaled = grad_rows * gain
    row_terms = ring_total(jnp.stack([jnp.sum(scaled, 1), jnp.sum(scaled * kept_hat, 1)]), "mp")
    row_terms = row_terms / full_width
    column_sums = jnp.stack([jnp.sum(grad_rows * kept_hat, 0), jnp.sum(grad_rows, 0)])
    columns = jnp.stack([stats[2], kept_inv, row_terms[0], row_terms[1]], 1)
    passed, outgoing = boundary(
        grad_rows, kept_rows, columns, gain, h_block(0), h_from_one, h_from_two,
        bias.reshape(col_count), section,
    )
    arrived = lax.all_to_all(outgoing, ("dp", "mp"), split_axis=0, concat_axis=0, tiled=True)

    weight_grad = None
    width = col_count // V_CHUNKS
    cuts = lambda value: [value[:, k * width:(k + 1) * width] for k in range(V_CHUNKS)]
    near3 = [along(part, OUTWARD) for part in lax.optimization_barrier(tuple(cuts(near1)))]
    ready = lax.optimization_barrier(
        (
            tuple(cuts(normed_kept)),
            tuple(cuts(jnp.where(inner, far1, near2))),
            tuple(cuts(jnp.where(inner, far2, far3))),
            tuple(cuts(near1)),
        )
    )
    for k in range(V_CHUNKS):
        last = near3[k]
        if weight_grad is not None:
            last, weight_grad = lax.optimization_barrier((last, weight_grad))
        own, one, three, near = (part[k] for part in ready)
        kept_all = jnp.concatenate([own, one, jnp.where(inner, near, last), three])
        weight_grad = grad_block(kept_all, c_all, weight_grad, k, V_CHUNKS)
        if k == V_CHUNKS // 2 - 1:
            arrived, column_sums, weight_grad = lax.optimization_barrier(
                (arrived, column_sums, weight_grad)
            )

    column_parts = lax.all_gather(column_sums, "dp", axis=0)
    column_grads = column_parts[0] + column_parts[1] + column_parts[2] + column_parts[3]
    arrived = flip(arrived, "section", 1)
    next_in = jnp.where(section == 0, matrix_of(arrived, 4, False), matrix_of(arrived, 4, True))

    return (
        next_in.reshape(fwd_in.shape),
        passed.reshape(fwd_in.shape),
        weight_grad.reshape(weight.shape),
        bias_grad.reshape(1, col_count),
        column_grads.reshape(1, 2, col_count),
    )


def shards(*arrays):
    if lax.axis_size("dp") == 4 and lax.axis_size("mp") == 4:
        return shards_of_four(*arrays)
    return shards_of_any_size(*arrays)


def solution(mesh):
    placed = (
        P("section", "dp", "mp", None, None),
        P("section", "dp", "mp", None, None),
        P("section", "dp", "mp", None, None),
        P("section", "mp", "dp"),
        P("section", "dp"),
        P("section", "mp"),
        P("section", "mp"),
    )
    return jax.shard_map(
        shards,
        mesh=mesh,
        in_specs=placed,
        out_specs=(
            P("section", "dp", "mp", None, None),
            P("section", "dp", "mp", None, None),
            P("section", "mp", "dp"),
            P("section", "dp"),
            P("section", None, "mp"),
        ),
        check_vma=False,
    )
```

```python
import functools

import jax
import jax.numpy as jnp
from jax import lax
from jax.experimental import pallas as pl
from jax.experimental.pallas import tpu as pltpu
from jax.sharding import PartitionSpec as P

eps = 1e-05
LIGHT = pl.CostEstimate(flops=1, bytes_accessed=1, transcendentals=0)


def flip(value, axis, mask):
    n = lax.axis_size(axis)
    return lax.ppermute(value, axis, [(s, s ^ mask) for s in range(n)])


def grad_kernel(v_ref, c_ref, *rest):
    out_ref, turned = rest[-2:]

    @pl.when(pl.program_id(0) == 0)
    def _():
        turned[...] = v_ref[...].T

    out_ref[...] = jnp.dot(turned[...], c_ref[...], preferred_element_type=jnp.float32)


def grad_block(kept_block, upstream, filled, block, blocks):
    tokens, width = kept_block.shape
    cols = upstream.shape[1]
    step = 768
    specs = [
        pl.BlockSpec((tokens, width), lambda j: (0, 0)),
        pl.BlockSpec((tokens, step), lambda j: (0, j)),
    ]
    operands = [kept_block, upstream]
    aliases = {}
    if filled is not None:
        specs.append(pl.BlockSpec(memory_space=pl.ANY))
        operands.append(filled)
        aliases = {2: 0}
    return pl.pallas_call(
        grad_kernel,
        grid=(cols // step,),
        in_specs=specs,
        out_specs=pl.BlockSpec((width, step), lambda j: (block, j)),
        out_shape=jax.ShapeDtypeStruct((width * blocks, cols), jnp.float32),
        scratch_shapes=[pltpu.VMEM((width, tokens), jnp.bfloat16)],
        input_output_aliases=aliases,
        compiler_params=pltpu.CompilerParams(vmem_limit_bytes=32 * 2**20),
        cost_estimate=LIGHT,
    )(*operands)


def share_kernel(count, turned, *refs):
    w_ref, out_ref = refs[2 * count], refs[-1]
    half = refs[0].shape[1]
    for k in range(count):
        total = None
        for side in range(2):
            cut = pl.ds(side * half, half)
            part = lax.dot_general(
                refs[2 * k + side][...],
                w_ref[:, cut] if turned else w_ref[cut, :],
                (((1,), (1 if turned else 0,)), ((), ())),
                preferred_element_type=jnp.float32,
            )
            total = part if total is None else total + part
        out_ref[k] = total.astype(jnp.bfloat16)


def shares(blocks, w, turned, filled, at, total):
    count = len(blocks)
    halves = []
    for block in blocks:
        halves += list(block) if isinstance(block, tuple) else [(block, 0), (block, 1)]
    rows = halves[0][0].shape[0]
    depth = w.shape[1] if turned else w.shape[0]
    cols = w.shape[0] if turned else w.shape[1]
    step = 512
    specs = [
        pl.BlockSpec((rows, depth // 2), functools.partial(lambda side, j: (0, side), side))
        for array, side in halves
    ]
    if turned:
        specs.append(pl.BlockSpec((step, depth), lambda j: (j, 0)))
    else:
        specs.append(pl.BlockSpec((depth, step), lambda j: (0, j)))
    operands = [array for array, side in halves] + [w]
    aliases = {}
    if filled is not None:
        specs.append(pl.BlockSpec(memory_space=pl.ANY))
        operands.append(filled)
        aliases = {2 * count + 1: 0}
    return pl.pallas_call(
        functools.partial(share_kernel, count, turned),
        grid=(cols // step,),
        in_specs=specs,
        out_specs=pl.BlockSpec((count, rows, step), lambda j: (at // count, 0, j)),
        out_shape=jax.ShapeDtypeStruct((total, rows, cols), jnp.bfloat16),
        input_output_aliases=aliases,
        compiler_params=pltpu.CompilerParams(vmem_limit_bytes=32 * 2**20),
        cost_estimate=LIGHT,
    )(*operands)


def boundary_kernel(upper_ref, lower_ref, kept_ref, columns_ref, gain_ref, h_ref, bias_ref, section_ref, passed_ref, out_ref):
    step = pl.program_id(0)
    first = section_ref[0] == 0
    groups = pl.num_programs(0)
    width = out_ref.shape[2]
    f32 = jnp.float32
    columns = columns_ref[...]
    mean, inverse, one, two = (columns[:, k:k + 1] for k in range(4))
    for f in range(out_ref.shape[0] // 4):
        cut = pl.ds(f * width, width)
        hat = (kept_ref[:, cut].astype(f32) - mean) * inverse
        rows = jnp.where(step < 2, upper_ref[:, cut], lower_ref[:, cut])
        grad = (inverse * (rows * gain_ref[:, cut] - one - hat * two)).astype(jnp.bfloat16)
        output = (h_ref[:, cut].astype(f32) + bias_ref[:, cut]).astype(jnp.bfloat16)
        passed_ref[:, cut] = jnp.where(first, grad, output)
        out_ref[jnp.where(first, step * groups + f, f * groups + step)] = jnp.where(
            first, output, grad
        )


def boundary(upper, lower, kept_rows, columns, gain, summed, bias, section):
    rows, cols = kept_rows.shape
    part = rows // 4
    wide = pl.BlockSpec((part, cols), lambda j: (j, 0))
    line = pl.BlockSpec((1, cols), lambda j: (0, 0))
    return pl.pallas_call(
        boundary_kernel,
        grid=(4,),
        in_specs=[
            pl.BlockSpec((part, cols), lambda j: (jnp.minimum(j, 1), 0)),
            pl.BlockSpec((part, cols), lambda j: (jnp.maximum(j - 2, 0), 0)),
            wide, pl.BlockSpec((part, 4), lambda j: (j, 0)), line, wide, line,
            pl.BlockSpec(memory_space=pltpu.SMEM),
        ],
        out_specs=[wide, pl.BlockSpec((16, part, cols // 4), lambda j: (0, 0, 0))],
        out_shape=[
            jax.ShapeDtypeStruct((rows, cols), jnp.bfloat16),
            jax.ShapeDtypeStruct((16, part, cols // 4), jnp.bfloat16),
        ],
        compiler_params=pltpu.CompilerParams(vmem_limit_bytes=32 * 2**20),
        cost_estimate=LIGHT,
    )(
        upper, lower, kept_rows, columns, gain.reshape(1, cols), summed, bias.reshape(1, cols),
        section.reshape(1),
    )


def joined_kernel(pieces_ref, section_ref, out_ref):
    step = pl.program_id(0)
    width = pieces_ref.shape[2]
    for c in range(4):
        piece = jnp.where(section_ref[0] == 0, step * 4 + c, c * 4 + step)
        out_ref[:, pl.ds(c * width, width)] = pieces_ref[piece]


def joined(pieces, section):
    count, part, width = pieces.shape
    return pl.pallas_call(
        joined_kernel,
        grid=(4,),
        in_specs=[
            pl.BlockSpec((count, part, width), lambda j: (0, 0, 0)),
            pl.BlockSpec(memory_space=pltpu.SMEM),
        ],
        out_specs=pl.BlockSpec((part, 4 * width), lambda j: (j, 0)),
        out_shape=jax.ShapeDtypeStruct((4 * part, 4 * width), pieces.dtype),
        compiler_params=pltpu.CompilerParams(vmem_limit_bytes=32 * 2**20),
        cost_estimate=LIGHT,
    )(pieces, section.reshape(1))


def from_partner(value, axis, stride):
    mask = 2**stride
    pairs = [(source, source ^ mask) for source in range(lax.axis_size(axis))]
    return lax.ppermute(value, axis, pairs)


def standardize(values, totals, squares, full_width):
    mean_val = totals / full_width
    spread = squares / full_width - mean_val * mean_val
    inv_std = lax.rsqrt(spread + eps)
    return ((values - mean_val[:, None]) * inv_std[:, None], inv_std)


def regroup(outgoing, groups):
    flat_buffer = outgoing.reshape((groups * groups,) + outgoing.shape[2:])
    moved_data = lax.all_to_all(flat_buffer, ("dp", "mp"), split_axis=0, concat_axis=0, tiled=True)
    return moved_data.reshape(outgoing.shape)


def shards_of_any_size(fwd_in, kept_in, cotangent, weight, bias, norm_gain, norm_shift):
    section_index = lax.axis_index("section")
    groups = lax.axis_size("dp")
    row_count = fwd_in.shape[3]
    col_count = fwd_in.shape[4]
    full_width = col_count * lax.axis_size("mp")
    piece_rows = row_count // groups
    piece_cols = col_count // groups
    weight_tile = weight.reshape(col_count, col_count)
    gain_cols = norm_gain.reshape(col_count)
    shift_cols = norm_shift.reshape(col_count)
    fresh_rows = fwd_in.reshape(row_count, col_count).astype(jnp.float32)
    kept_values = kept_in.reshape(row_count, col_count).astype(jnp.float32)
    upstream = cotangent.reshape(row_count, col_count)
    row_stats = lax.psum(
        (
            jnp.sum(fresh_rows, 1),
            jnp.sum(fresh_rows * fresh_rows, 1),
            jnp.sum(kept_values, 1),
            jnp.sum(kept_values * kept_values, 1),
        ),
        "mp",
    )
    fresh_hat, unused_scale = standardize(fresh_rows, row_stats[0], row_stats[1], full_width)
    kept_hat, kept_inv = standardize(kept_values, row_stats[2], row_stats[3], full_width)
    normed = (fresh_hat * gain_cols + shift_cols).astype(jnp.bfloat16)
    normed_kept = (kept_hat * gain_cols + shift_cols).astype(jnp.bfloat16)
    upstream_all = lax.all_gather(upstream, "mp", axis=0, tiled=True)
    gathered, gathered_kept = (
        lax.all_gather(normed, "dp", axis=0, tiled=True),
        lax.all_gather(normed_kept, "dp", axis=0, tiled=True),
    )
    weight_grad = lax.dot_general(
        gathered_kept, upstream_all, (((0,), (0,)), ((), ())), preferred_element_type=jnp.float32
    )
    segment = gathered
    summed = lax.psum_scatter(
        jnp.dot(segment, weight_tile, preferred_element_type=jnp.float32).astype(jnp.bfloat16),
        "mp",
        scatter_dimension=0,
        tiled=True,
    ).astype(jnp.float32)
    output = (summed + bias.reshape(col_count)).astype(jnp.bfloat16)
    bias_grad = jnp.sum(upstream_all, 0, dtype=jnp.float32)
    segment = upstream_all
    grad_rows = lax.psum_scatter(
        lax.dot_general(
            segment, weight_tile, (((1,), (1,)), ((), ())), preferred_element_type=jnp.float32
        ).astype(jnp.bfloat16),
        "dp",
        scatter_dimension=0,
        tiled=True,
    ).astype(jnp.float32)
    scaled = grad_rows * gain_cols
    column_grads = lax.psum((jnp.sum(grad_rows * kept_hat, 0), jnp.sum(grad_rows, 0)), "dp")
    row_terms = lax.psum((jnp.sum(scaled, 1), jnp.sum(scaled * kept_hat, 1)), "mp")
    input_grad = (
        kept_inv[:, None]
        * (
            scaled
            - row_terms[0][:, None] / full_width
            - kept_hat * (row_terms[1][:, None] / full_width)
        )
    ).astype(jnp.bfloat16)
    out_pack = output.reshape(groups, piece_rows, groups, piece_cols).transpose(0, 2, 1, 3)
    grad_pack = input_grad.reshape(groups, piece_rows, groups, piece_cols).transpose(2, 0, 1, 3)
    outgoing = jnp.where(section_index == 0, out_pack, grad_pack)
    arrived = from_partner(regroup(outgoing, groups), "section", 0)
    as_cotangent = arrived.transpose(0, 2, 1, 3).reshape(row_count, col_count)
    as_input = arrived.transpose(1, 2, 0, 3).reshape(row_count, col_count)
    next_in = jnp.where(section_index == 0, as_cotangent, as_input)
    passed = jnp.where(section_index == 0, input_grad, output)
    return (
        next_in.reshape(fwd_in.shape),
        passed.reshape(fwd_in.shape),
        weight_grad.reshape(1, col_count, col_count),
        bias_grad.reshape(1, col_count),
        jnp.stack([column_grads[0], column_grads[1]]).reshape(1, 2, col_count),
    )


PAIRS = [(0, 1), (1, 0), (2, 3), (3, 2)]
MIDDLE = [(1, 2), (2, 1)]
INWARD = [(0, 1), (3, 2)]
OUTWARD = [(1, 0), (2, 3)]


def shards_of_four(fwd_in, kept_in, cotangent, weight, bias, norm_gain, norm_shift):
    f32, bf16 = jnp.float32, jnp.bfloat16
    section = lax.axis_index("section")
    dp, mp = lax.axis_index("dp"), lax.axis_index("mp")
    inner = (dp == 1) | (dp == 2)
    row_count, col_count = fwd_in.shape[3], fwd_in.shape[4]
    full_width = col_count * 4
    half = col_count // 2
    w = weight.reshape(weight.shape[1], weight.shape[2])
    gain = norm_gain.reshape(col_count)
    shift = norm_shift.reshape(col_count)
    fresh_rows = fwd_in.reshape(row_count, col_count)
    kept_rows = kept_in.reshape(row_count, col_count)
    upstream = cotangent.reshape(row_count, col_count)
    along = lambda value, pairs: lax.ppermute(value, "dp", pairs)
    pick = lambda stack, k: lax.dynamic_index_in_dim(stack, k, 0, keepdims=False)

    def standardize(values, mean, square_mean):
        inverse = lax.rsqrt(square_mean - mean * mean + eps)
        return (values.astype(f32) - mean[:, None]) * inverse[:, None], inverse

    def affine(hat):
        return (hat * gain + shift).astype(bf16)

    def added(one, two):
        return (one.astype(f32) + two.astype(f32)).astype(bf16)

    seq = lambda *values: lax.optimization_barrier(values)

    u1a, u1b = along(fresh_rows, PAIRS), along(fresh_rows, MIDDLE)
    c_left, c_right = upstream[:, :half], upstream[:, half:]
    c1_left, c2_right = flip(c_left, "mp", 1), flip(c_right, "mp", 2)
    fresh, kept = fresh_rows.astype(f32), kept_rows.astype(f32)
    sums = jnp.stack(
        [jnp.sum(fresh, 1), jnp.sum(fresh * fresh, 1), jnp.sum(kept, 1), jnp.sum(kept * kept, 1)]
    )
    other = flip(sums, "mp", 1)
    g_stack = shares([upstream], w, True, None, 3, 4)
    c1_left, c2_right, sums, other, g_stack = seq(c1_left, c2_right, sums, other, g_stack)
    c_from_one = flip(jnp.concatenate([c_right, c2_right], 1), "mp", 1)
    c_from_two = flip(jnp.concatenate([c_left, c1_left], 1), "mp", 2)
    sums = sums + other
    stats = (sums + flip(sums, "mp", 2)) / full_width
    kept_hat, kept_inv = standardize(kept_rows, stats[2], stats[3])
    normed_kept = affine(kept_hat)

    def normed(rows, row_stats):
        hat, unused = standardize(rows, row_stats[0], row_stats[1])
        return affine(hat)

    pair_stats = jnp.stack([stats[:2], along(stats[:2], PAIRS)])
    h_stack = shares([normed(fresh_rows, stats)], w, False, None, 0, 4)
    u1a, u1b, normed_kept, h_stack = seq(u1a, u1b, normed_kept, h_stack)

    sides = [slice(0, row_count // 2), slice(row_count // 2, row_count)]
    either = lambda from_inner, from_outer: jnp.where(inner, from_inner, from_outer)
    a1, b1, a2, b2, a3, b3, a4, b4, a5, b5, x2 = ([None, None] for unused in range(11))

    for k in range(2):
        a1[k] = along(either(u1b[sides[k]], normed_kept[sides[k]]), PAIRS)
        b1[k] = along(u1a[sides[k]], MIDDLE)
    h_stack = shares([normed(u1a, pair_stats[1])], w, False, h_stack, 1, 4)

    a1[0], b1[0], h_stack, c1_left, c2_right = seq(a1[0], b1[0], h_stack, c1_left, c2_right)
    a2[0], b2[0] = along(b1[0], OUTWARD), along(a1[0], MIDDLE)
    g_stack = shares(
        [((c1_left, 0), (c_from_one, 0)), ((c_from_two, 0), (c2_right, 0))], w, True, g_stack, 0, 4
    )
    a1[1], b1[1], g_stack = seq(a1[1], b1[1], g_stack)
    a2[1], b2[1] = along(b1[1], OUTWARD), along(a1[1], MIDDLE)
    pair_stats = seq(pair_stats, b1[1])[0]
    all_stats = jnp.concatenate([pair_stats, along(pair_stats, [(s, s ^ 2) for s in range(4)])])
    g_stack = shares([((c_from_two, 1), (c_from_one, 1))], w, True, g_stack, 2, 4)

    def g_block(k, side):
        apart = lax.bitwise_xor(lax.bitwise_xor(dp, mp), k)
        at = jnp.where(apart == 0, 3, apart - 1)
        return lax.dynamic_slice(
            g_stack, (at, side.start, 0), (1, side.stop - side.start, col_count)
        )[0]

    a2[0], b2[0], g_stack, normed_kept = seq(a2[0], b2[0], g_stack, normed_kept)
    sent, h_stack = seq(either(b2[0], g_block(3, sides[0])), h_stack)
    a3[0] = along(sent, PAIRS)
    b3[0] = along(normed_kept[sides[0]], MIDDLE)
    all_stats, h_stack = seq(all_stats, h_stack)
    u2 = jnp.where(inner, u1b, jnp.concatenate(a1))
    h_stack = shares([normed(u2, pick(all_stats, jnp.where(inner, 3, 2)))], w, False, h_stack, 2, 4)
    a2[1], b2[1], h_stack, normed_kept = seq(a2[1], b2[1], h_stack, normed_kept)
    sent, h_stack = seq(either(b2[1], g_block(3, sides[1])), h_stack)
    a3[1] = along(sent, PAIRS)
    b3[1] = along(normed_kept[sides[1]], MIDDLE)
    u3 = jnp.where(inner, jnp.concatenate(b1), jnp.concatenate(a2))
    h_stack = shares([normed(u3, pick(all_stats, jnp.where(inner, 2, 3)))], w, False, h_stack, 3, 4)

    nothing = jnp.zeros((row_count // 2, col_count), bf16)

    def fourth(k, chain):
        x2[k] = added(g_block(2, sides[k]), jnp.where(inner, a3[k], nothing))
        sent, x2[k], chain = seq(either(normed_kept[sides[k]], x2[k]), x2[k], chain)
        a4[k], b4[k] = along(sent, PAIRS), along(x2[k], MIDDLE)
        return chain

    a3[0], b3[0], h_stack = seq(a3[0], b3[0], h_stack)
    h_stack = fourth(0, h_stack)

    def h_block(b):
        apart = lax.bitwise_xor(dp, b)
        return pick(h_stack, jnp.where(inner & (apart >= 2), apart ^ 1, apart))

    h_all = jnp.concatenate([h_block(b) for b in range(4)])
    a3[1], b3[1], h_all = seq(a3[1], b3[1], h_all)
    summed = lax.psum_scatter(h_all, "mp", scatter_dimension=0, tiled=True)
    own_block = fourth(1, upstream)
    c_stack = jnp.stack(
        [
            own_block,
            jnp.concatenate([c1_left, c_from_one[:, :half]], 1),
            jnp.concatenate([c_from_two[:, :half], c2_right], 1),
            jnp.concatenate([c_from_two[:, half:], c_from_one[:, half:]], 1),
        ]
    )
    block_sums = jnp.sum(c_stack, 1, dtype=f32)
    in_order = [pick(block_sums, lax.bitwise_xor(mp, b)) for b in range(4)]
    bias_grad = in_order[0] + in_order[1] + in_order[2] + in_order[3]
    c_of = lambda k: pick(c_stack, lax.bitwise_xor(lax.bitwise_xor(dp, mp), k))
    c_all = jnp.concatenate(
        [c_of(0), c_of(1), c_of(jnp.where(inner, 3, 2)), c_of(jnp.where(inner, 2, 3))]
    )

    def fifth(k, chain):
        one, two, chain = seq(
            added(g_block(1, sides[k]), b4[k]), added(g_block(3, sides[k]), a4[k]), chain
        )
        a5[k], b5[k] = along(one, PAIRS), along(two, MIDDLE)
        return chain

    a4[0], b4[0], c_all = seq(a4[0], b4[0], c_all)
    c_all = fifth(0, c_all)
    a4[1], b4[1], c_all = seq(a4[1], b4[1], c_all)
    c_all = fifth(1, c_all)

    def gradient(k):
        rows = g_block(0, sides[k]).astype(f32) + a5[k].astype(f32) + b5[k].astype(f32)
        scaled, hat = rows * gain, kept_hat[sides[k]]
        return (
            rows,
            jnp.stack([jnp.sum(scaled, 1), jnp.sum(scaled * hat, 1)]),
            jnp.stack([jnp.sum(rows * hat, 0), jnp.sum(rows, 0)]),
        )

    near1 = jnp.concatenate(b3)
    a5[0], b5[0], near1, c_all = seq(a5[0], b5[0], near1, c_all)
    near3 = [along(near1[:, :half], OUTWARD), along(near1[:, half:], OUTWARD)]
    upper, upper_terms, upper_sums = gradient(0)
    a5[1], b5[1], upper_terms, upper_sums = seq(a5[1], b5[1], upper_terms, upper_sums)
    lower, lower_terms, lower_sums = gradient(1)
    row_terms = jnp.concatenate([upper_terms, lower_terms], 1)
    row_terms = row_terms + flip(row_terms, "mp", 1)
    row_terms = (row_terms + flip(row_terms, "mp", 2)) / full_width
    columns = jnp.stack([stats[2], kept_inv, row_terms[0], row_terms[1]], 1)
    passed, outgoing = boundary(
        upper, lower, kept_rows, columns, gain, summed, bias.reshape(col_count), section
    )
    arrived = lax.all_to_all(outgoing, ("dp", "mp"), split_axis=0, concat_axis=0, tiled=True)

    column_sums, c_all, outgoing = seq(upper_sums + lower_sums, c_all, outgoing)
    column_sums = column_sums + along(column_sums, PAIRS)
    column_grads = column_sums + along(column_sums, [(s, s ^ 2) for s in range(4)])
    width = half // 2
    early = [
        normed_kept,
        jnp.where(inner, jnp.concatenate(a1), jnp.concatenate(a4)),
        jnp.where(inner, jnp.concatenate(b2), jnp.concatenate(a3)),
    ]
    weight_grad = None
    for k in range(4):
        last = near3[k // 2]
        if weight_grad is None:
            last, c_all = seq(last, c_all)
        else:
            last, weight_grad = seq(last, weight_grad)
        cut = lambda value: value[:, k * width:(k + 1) * width]
        own, one, three = (cut(value) for value in early)
        two = jnp.where(inner, cut(near1), last[:, (k % 2) * width:(k % 2 + 1) * width])
        weight_grad = grad_block(
            jnp.concatenate([own, one, two, three]), c_all, weight_grad, k, 4
        )
        if k == 2:
            arrived, column_grads, weight_grad = seq(arrived, column_grads, weight_grad)
            arrived = flip(arrived, "section", 1)
    next_in = joined(arrived, section)

    return (
        next_in.reshape(fwd_in.shape),
        passed.reshape(fwd_in.shape),
        weight_grad.reshape(weight.shape),
        bias_grad.reshape(1, col_count),
        column_grads.reshape(1, 2, col_count),
    )


def shards(*arrays):
    if lax.axis_size("dp") == 4 and lax.axis_size("mp") == 4:
        return shards_of_four(*arrays)
    return shards_of_any_size(*arrays)


def solution(mesh):
    placed = (
        P("section", "dp", "mp", None, None),
        P("section", "dp", "mp", None, None),
        P("section", "dp", "mp", None, None),
        P("section", "mp", "dp"),
        P("section", "dp"),
        P("section", "mp"),
        P("section", "mp"),
    )
    return jax.shard_map(
        shards,
        mesh=mesh,
        in_specs=placed,
        out_specs=(
            P("section", "dp", "mp", None, None),
            P("section", "dp", "mp", None, None),
            P("section", "mp", "dp"),
            P("section", "dp"),
            P("section", None, "mp"),
        ),
        check_vma=False,
    )
```

```python
import functools

import jax
import jax.numpy as jnp
from jax import lax
from jax.experimental import pallas as pl
from jax.experimental.pallas import tpu as pltpu
from jax.sharding import PartitionSpec as P

eps = 1e-05
LIGHT = pl.CostEstimate(flops=1, bytes_accessed=1, transcendentals=0)


def flip(value, axis, mask):
    n = lax.axis_size(axis)
    return lax.ppermute(value, axis, [(s, s ^ mask) for s in range(n)])


def grad_kernel(v_ref, c_ref, *rest):
    out_ref, turned = rest[-2:]

    @pl.when(pl.program_id(0) == 0)
    def _():
        turned[...] = v_ref[...].T

    out_ref[...] = jnp.dot(turned[...], c_ref[...], preferred_element_type=jnp.float32)


def grad_block(kept_block, upstream, filled, block, blocks):
    tokens, width = kept_block.shape
    cols = upstream.shape[1]
    step = 768
    specs = [
        pl.BlockSpec((tokens, width), lambda j: (0, 0)),
        pl.BlockSpec((tokens, step), lambda j: (0, j)),
    ]
    operands = [kept_block, upstream]
    aliases = {}
    if filled is not None:
        specs.append(pl.BlockSpec(memory_space=pl.ANY))
        operands.append(filled)
        aliases = {2: 0}
    return pl.pallas_call(
        grad_kernel,
        grid=(cols // step,),
        in_specs=specs,
        out_specs=pl.BlockSpec((width, step), lambda j: (block, j)),
        out_shape=jax.ShapeDtypeStruct((width * blocks, cols), jnp.float32),
        scratch_shapes=[pltpu.VMEM((width, tokens), jnp.bfloat16)],
        input_output_aliases=aliases,
        compiler_params=pltpu.CompilerParams(vmem_limit_bytes=32 * 2**20),
        cost_estimate=LIGHT,
    )(*operands)


def share_kernel(count, turned, *refs):
    w_ref, out_ref = refs[2 * count], refs[-1]
    half = refs[0].shape[1]
    for k in range(count):
        total = None
        for side in range(2):
            cut = pl.ds(side * half, half)
            part = lax.dot_general(
                refs[2 * k + side][...],
                w_ref[:, cut] if turned else w_ref[cut, :],
                (((1,), (1 if turned else 0,)), ((), ())),
                preferred_element_type=jnp.float32,
            )
            total = part if total is None else total + part
        out_ref[k] = total.astype(jnp.bfloat16)


def shares(blocks, w, turned, filled, place, total, total_rows):
    count = len(blocks)
    halves = []
    for block in blocks:
        halves += list(block) if isinstance(block, tuple) else [(block, 0, 0), (block, 1, 0)]
    rows = total_rows // total
    depth = w.shape[1] if turned else w.shape[0]
    cols = w.shape[0] if turned else w.shape[1]
    step = 512
    specs = [
        pl.BlockSpec((rows, depth // 2), functools.partial(lambda side, at, j: (at, side), side, at))
        for array, side, at in halves
    ]
    if turned:
        specs.append(pl.BlockSpec((step, depth), lambda j: (j, 0)))
    else:
        specs.append(pl.BlockSpec((depth, step), lambda j: (0, j)))
    operands = [array for array, side, at in halves] + [w]
    aliases = {}
    if filled is not None:
        specs.append(pl.BlockSpec(memory_space=pl.ANY))
        operands.append(filled)
        aliases = {2 * count + 1: 0}
    return pl.pallas_call(
        functools.partial(share_kernel, count, turned),
        grid=(cols // step,),
        in_specs=specs,
        out_specs=pl.BlockSpec((count, rows, step), lambda j: (place // count, 0, j)),
        out_shape=jax.ShapeDtypeStruct((total, rows, cols), jnp.bfloat16),
        input_output_aliases=aliases,
        compiler_params=pltpu.CompilerParams(vmem_limit_bytes=32 * 2**20),
        cost_estimate=LIGHT,
    )(*operands)


def normed_kernel(rows_ref, stats_ref, gain_ref, shift_ref, out_ref):
    stats = stats_ref[...]
    hat = (rows_ref[...].astype(jnp.float32) - stats[:, 0:1]) * stats[:, 1:2]
    out_ref[...] = (hat * gain_ref[...] + shift_ref[...]).astype(jnp.bfloat16)


def normed(rows, row_stats, gain, shift):
    mean, square_mean = row_stats[0], row_stats[1]
    stats = jnp.stack([mean, lax.rsqrt(square_mean - mean * mean + eps)], 1)
    count, cols = rows.shape
    part = 64
    line = pl.BlockSpec((1, cols), lambda j: (0, 0))
    wide = pl.BlockSpec((part, cols), lambda j: (j, 0))
    return pl.pallas_call(
        normed_kernel,
        grid=(count // part,),
        in_specs=[wide, pl.BlockSpec((part, 2), lambda j: (j, 0)), line, line],
        out_specs=wide,
        out_shape=jax.ShapeDtypeStruct((count, cols), jnp.bfloat16),
        compiler_params=pltpu.CompilerParams(vmem_limit_bytes=32 * 2**20),
        cost_estimate=LIGHT,
    )(rows, stats, gain.reshape(1, cols), shift.reshape(1, cols))


def reorder_kernel(order_ref, stack_ref, out_ref):
    out_ref[...] = stack_ref[...]


def reorder(stack, order):
    count, rows, cols = stack.shape
    out = pl.pallas_call(
        reorder_kernel,
        grid_spec=pltpu.PrefetchScalarGridSpec(
            num_scalar_prefetch=1,
            grid=(count,),
            in_specs=[pl.BlockSpec((1, rows, cols), lambda j, order: (order[j], 0, 0))],
            out_specs=pl.BlockSpec((1, rows, cols), lambda j, order: (j, 0, 0)),
        ),
        out_shape=jax.ShapeDtypeStruct(stack.shape, stack.dtype),
        compiler_params=pltpu.CompilerParams(vmem_limit_bytes=32 * 2**20),
        cost_estimate=LIGHT,
    )(jnp.stack(order).astype(jnp.int32), stack)
    return out.reshape(count * rows, cols)


def boundary_kernel(upper_ref, lower_ref, kept_ref, columns_ref, gain_ref, h_ref, bias_ref, section_ref, passed_ref, out_ref):
    step = pl.program_id(0)
    first = section_ref[0] == 0
    groups = pl.num_programs(0)
    width = out_ref.shape[2]
    f32 = jnp.float32
    columns = columns_ref[...]
    mean, inverse, one, two = (columns[:, k:k + 1] for k in range(4))
    for f in range(out_ref.shape[0] // 4):
        cut = pl.ds(f * width, width)
        hat = (kept_ref[:, cut].astype(f32) - mean) * inverse
        rows = jnp.where(step < 2, upper_ref[:, cut], lower_ref[:, cut])
        grad = (inverse * (rows * gain_ref[:, cut] - one - hat * two)).astype(jnp.bfloat16)
        output = (h_ref[:, cut].astype(f32) + bias_ref[:, cut]).astype(jnp.bfloat16)
        passed_ref[:, cut] = jnp.where(first, grad, output)
        out_ref[jnp.where(first, step * groups + f, f * groups + step)] = jnp.where(
            first, output, grad
        )


def boundary(upper, lower, kept_rows, columns, gain, summed, bias, section):
    rows, cols = kept_rows.shape
    part = rows // 4
    wide = pl.BlockSpec((part, cols), lambda j: (j, 0))
    line = pl.BlockSpec((1, cols), lambda j: (0, 0))
    return pl.pallas_call(
        boundary_kernel,
        grid=(4,),
        in_specs=[
            pl.BlockSpec((part, cols), lambda j: (jnp.minimum(j, 1), 0)),
            pl.BlockSpec((part, cols), lambda j: (jnp.maximum(j - 2, 0), 0)),
            wide, pl.BlockSpec((part, 4), lambda j: (j, 0)), line, wide, line,
            pl.BlockSpec(memory_space=pltpu.SMEM),
        ],
        out_specs=[wide, pl.BlockSpec((16, part, cols // 4), lambda j: (0, 0, 0))],
        out_shape=[
            jax.ShapeDtypeStruct((rows, cols), jnp.bfloat16),
            jax.ShapeDtypeStruct((16, part, cols // 4), jnp.bfloat16),
        ],
        compiler_params=pltpu.CompilerParams(vmem_limit_bytes=32 * 2**20),
        cost_estimate=LIGHT,
    )(
        upper, lower, kept_rows, columns, gain.reshape(1, cols), summed, bias.reshape(1, cols),
        section.reshape(1),
    )


def joined_kernel(pieces_ref, section_ref, out_ref):
    step = pl.program_id(0)
    width = pieces_ref.shape[2]
    for c in range(4):
        piece = jnp.where(section_ref[0] == 0, step * 4 + c, c * 4 + step)
        out_ref[:, pl.ds(c * width, width)] = pieces_ref[piece]


def joined(pieces, section):
    count, part, width = pieces.shape
    return pl.pallas_call(
        joined_kernel,
        grid=(4,),
        in_specs=[
            pl.BlockSpec((count, part, width), lambda j: (0, 0, 0)),
            pl.BlockSpec(memory_space=pltpu.SMEM),
        ],
        out_specs=pl.BlockSpec((part, 4 * width), lambda j: (j, 0)),
        out_shape=jax.ShapeDtypeStruct((4 * part, 4 * width), pieces.dtype),
        compiler_params=pltpu.CompilerParams(vmem_limit_bytes=32 * 2**20),
        cost_estimate=LIGHT,
    )(pieces, section.reshape(1))


def from_partner(value, axis, stride):
    mask = 2**stride
    pairs = [(source, source ^ mask) for source in range(lax.axis_size(axis))]
    return lax.ppermute(value, axis, pairs)


def standardize(values, totals, squares, full_width):
    mean_val = totals / full_width
    spread = squares / full_width - mean_val * mean_val
    inv_std = lax.rsqrt(spread + eps)
    return ((values - mean_val[:, None]) * inv_std[:, None], inv_std)


def regroup(outgoing, groups):
    flat_buffer = outgoing.reshape((groups * groups,) + outgoing.shape[2:])
    moved_data = lax.all_to_all(flat_buffer, ("dp", "mp"), split_axis=0, concat_axis=0, tiled=True)
    return moved_data.reshape(outgoing.shape)


def shards_of_any_size(fwd_in, kept_in, cotangent, weight, bias, norm_gain, norm_shift):
    section_index = lax.axis_index("section")
    groups = lax.axis_size("dp")
    row_count = fwd_in.shape[3]
    col_count = fwd_in.shape[4]
    full_width = col_count * lax.axis_size("mp")
    piece_rows = row_count // groups
    piece_cols = col_count // groups
    weight_tile = weight.reshape(col_count, col_count)
    gain_cols = norm_gain.reshape(col_count)
    shift_cols = norm_shift.reshape(col_count)
    fresh_rows = fwd_in.reshape(row_count, col_count).astype(jnp.float32)
    kept_values = kept_in.reshape(row_count, col_count).astype(jnp.float32)
    upstream = cotangent.reshape(row_count, col_count)
    row_stats = lax.psum(
        (
            jnp.sum(fresh_rows, 1),
            jnp.sum(fresh_rows * fresh_rows, 1),
            jnp.sum(kept_values, 1),
            jnp.sum(kept_values * kept_values, 1),
        ),
        "mp",
    )
    fresh_hat, unused_scale = standardize(fresh_rows, row_stats[0], row_stats[1], full_width)
    kept_hat, kept_inv = standardize(kept_values, row_stats[2], row_stats[3], full_width)
    normed = (fresh_hat * gain_cols + shift_cols).astype(jnp.bfloat16)
    normed_kept = (kept_hat * gain_cols + shift_cols).astype(jnp.bfloat16)
    upstream_all = lax.all_gather(upstream, "mp", axis=0, tiled=True)
    gathered, gathered_kept = (
        lax.all_gather(normed, "dp", axis=0, tiled=True),
        lax.all_gather(normed_kept, "dp", axis=0, tiled=True),
    )
    weight_grad = lax.dot_general(
        gathered_kept, upstream_all, (((0,), (0,)), ((), ())), preferred_element_type=jnp.float32
    )
    segment = gathered
    summed = lax.psum_scatter(
        jnp.dot(segment, weight_tile, preferred_element_type=jnp.float32).astype(jnp.bfloat16),
        "mp",
        scatter_dimension=0,
        tiled=True,
    ).astype(jnp.float32)
    output = (summed + bias.reshape(col_count)).astype(jnp.bfloat16)
    bias_grad = jnp.sum(upstream_all, 0, dtype=jnp.float32)
    segment = upstream_all
    grad_rows = lax.psum_scatter(
        lax.dot_general(
            segment, weight_tile, (((1,), (1,)), ((), ())), preferred_element_type=jnp.float32
        ).astype(jnp.bfloat16),
        "dp",
        scatter_dimension=0,
        tiled=True,
    ).astype(jnp.float32)
    scaled = grad_rows * gain_cols
    column_grads = lax.psum((jnp.sum(grad_rows * kept_hat, 0), jnp.sum(grad_rows, 0)), "dp")
    row_terms = lax.psum((jnp.sum(scaled, 1), jnp.sum(scaled * kept_hat, 1)), "mp")
    input_grad = (
        kept_inv[:, None]
        * (
            scaled
            - row_terms[0][:, None] / full_width
            - kept_hat * (row_terms[1][:, None] / full_width)
        )
    ).astype(jnp.bfloat16)
    out_pack = output.reshape(groups, piece_rows, groups, piece_cols).transpose(0, 2, 1, 3)
    grad_pack = input_grad.reshape(groups, piece_rows, groups, piece_cols).transpose(2, 0, 1, 3)
    outgoing = jnp.where(section_index == 0, out_pack, grad_pack)
    arrived = from_partner(regroup(outgoing, groups), "section", 0)
    as_cotangent = arrived.transpose(0, 2, 1, 3).reshape(row_count, col_count)
    as_input = arrived.transpose(1, 2, 0, 3).reshape(row_count, col_count)
    next_in = jnp.where(section_index == 0, as_cotangent, as_input)
    passed = jnp.where(section_index == 0, input_grad, output)
    return (
        next_in.reshape(fwd_in.shape),
        passed.reshape(fwd_in.shape),
        weight_grad.reshape(1, col_count, col_count),
        bias_grad.reshape(1, col_count),
        jnp.stack([column_grads[0], column_grads[1]]).reshape(1, 2, col_count),
    )


PAIRS = [(0, 1), (1, 0), (2, 3), (3, 2)]
MIDDLE = [(1, 2), (2, 1)]
INWARD = [(0, 1), (3, 2)]
OUTWARD = [(1, 0), (2, 3)]


def shards_of_four(fwd_in, kept_in, cotangent, weight, bias, norm_gain, norm_shift):
    f32, bf16 = jnp.float32, jnp.bfloat16
    section = lax.axis_index("section")
    dp, mp = lax.axis_index("dp"), lax.axis_index("mp")
    inner = (dp == 1) | (dp == 2)
    row_count, col_count = fwd_in.shape[3], fwd_in.shape[4]
    full_width = col_count * 4
    half = col_count // 2
    w = weight.reshape(weight.shape[1], weight.shape[2])
    gain = norm_gain.reshape(col_count)
    shift = norm_shift.reshape(col_count)
    fresh_rows = fwd_in.reshape(row_count, col_count)
    kept_rows = kept_in.reshape(row_count, col_count)
    upstream = cotangent.reshape(row_count, col_count)
    along = lambda value, pairs: lax.ppermute(value, "dp", pairs)
    pick = lambda stack, k: lax.dynamic_index_in_dim(stack, k, 0, keepdims=False)

    def standardize(values, mean, square_mean):
        inverse = lax.rsqrt(square_mean - mean * mean + eps)
        return (values.astype(f32) - mean[:, None]) * inverse[:, None], inverse

    def added(one, two):
        return (one.astype(f32) + two.astype(f32)).astype(bf16)

    seq = lambda *values: lax.optimization_barrier(values)

    sides = [slice(0, row_count // 2), slice(row_count // 2, row_count)]
    either = lambda from_inner, from_outer: jnp.where(inner, from_inner, from_outer)
    u1a, u1b, a1, b1, a2, b2, a3, b3, a4, b4, a5, b5, x2 = (
        [None, None] for unused in range(13)
    )

    c_all = lax.all_gather(upstream, "mp", axis=0, tiled=True)
    for k in range(2):
        u1a[k] = along(fresh_rows[sides[k]], PAIRS)
        u1b[k] = along(fresh_rows[sides[k]], MIDDLE)
    fresh, kept = fresh_rows.astype(f32), kept_rows.astype(f32)
    sums = jnp.stack(
        [jnp.sum(fresh, 1), jnp.sum(fresh * fresh, 1), jnp.sum(kept, 1), jnp.sum(kept * kept, 1)]
    )
    u1a[0], u1b[0], sums = seq(u1a[0], u1b[0], sums)
    sums = sums + flip(sums, "mp", 1)
    stats = (sums + flip(sums, "mp", 2)) / full_width
    kept_hat, kept_inv = standardize(kept_rows, stats[2], stats[3])
    normed_kept = normed(kept_rows, stats[2:], gain, shift)

    u1a[0], u1b[0], normed_kept, stats = seq(u1a[0], u1b[0], normed_kept, stats)
    pair_stats = jnp.stack([stats[:2], along(stats[:2], PAIRS)])
    sent, stats = seq(either(u1b[0], normed_kept[sides[0]]), stats)
    a1[0], b1[0] = along(sent, PAIRS), along(u1a[0], MIDDLE)
    u1a[1], u1b[1], normed_kept, stats = seq(u1a[1], u1b[1], normed_kept, stats)
    sent, stats = seq(either(u1b[1], normed_kept[sides[1]]), stats)
    a1[1], b1[1] = along(sent, PAIRS), along(u1a[1], MIDDLE)
    pair_stats, stats, u1a[1] = seq(pair_stats, stats, u1a[1])
    h_stack = shares(
        [
            normed(fresh_rows, stats, gain, shift),
            normed(jnp.concatenate(u1a), pair_stats[1], gain, shift),
        ],
        w, False, None, 0, 4, 4 * row_count,
    )

    a1[0], b1[0], h_stack, pair_stats = seq(a1[0], b1[0], h_stack, pair_stats)
    a2[0], b2[0] = along(b1[0], OUTWARD), along(a1[0], MIDDLE)
    all_stats = jnp.concatenate([pair_stats, along(pair_stats, [(s, s ^ 2) for s in range(4)])])
    a1[1], b1[1], h_stack, all_stats, c_all = seq(a1[1], b1[1], h_stack, all_stats, c_all)
    a2[1], b2[1] = along(b1[1], OUTWARD), along(a1[1], MIDDLE)
    g_stack = None
    for first in (0, 2):
        blocks = [((c_all, 0, b), (c_all, 1, b)) for b in (first, first + 1)]
        g_stack = shares(blocks, w, True, g_stack, first, 4, 4 * row_count)

    def g_block(k, side):
        return lax.dynamic_slice(
            g_stack, (dp ^ k, side.start, 0), (1, side.stop - side.start, col_count)
        )[0]

    a2[0], b2[0], g_stack, normed_kept = seq(a2[0], b2[0], g_stack, normed_kept)
    sent, g_stack = seq(either(b2[0], g_block(3, sides[0])), g_stack)
    a3[0], b3[0] = along(sent, PAIRS), along(normed_kept[sides[0]], MIDDLE)
    a2[1], b2[1], g_stack, normed_kept = seq(a2[1], b2[1], g_stack, normed_kept)
    sent, h_stack = seq(either(b2[1], g_block(3, sides[1])), h_stack)
    a3[1], b3[1] = along(sent, PAIRS), along(normed_kept[sides[1]], MIDDLE)
    u2 = jnp.where(inner, jnp.concatenate(u1b), jnp.concatenate(a1))
    u3 = jnp.where(inner, jnp.concatenate(b1), jnp.concatenate(a2))
    h_stack = shares(
        [
            normed(u2, pick(all_stats, jnp.where(inner, 3, 2)), gain, shift),
            normed(u3, pick(all_stats, jnp.where(inner, 2, 3)), gain, shift),
        ],
        w, False, h_stack, 2, 4, 4 * row_count,
    )

    nothing = jnp.zeros((row_count // 2, col_count), bf16)

    def fourth(k, chain):
        x2[k] = added(g_block(2, sides[k]), jnp.where(inner, a3[k], nothing))
        sent, x2[k], chain = seq(either(normed_kept[sides[k]], x2[k]), x2[k], chain)
        a4[k], b4[k] = along(sent, PAIRS), along(x2[k], MIDDLE)
        return chain

    a3[0], b3[0], h_stack = seq(a3[0], b3[0], h_stack)
    h_stack = fourth(0, h_stack)

    places = [lax.bitwise_xor(dp, b) for b in range(4)]
    places = [jnp.where(inner & (at >= 2), at ^ 1, at) for at in places]
    h_all = reorder(h_stack, places)
    a3[1], b3[1], h_all = seq(a3[1], b3[1], h_all)
    summed = lax.psum_scatter(h_all, "mp", scatter_dimension=0, tiled=True)
    c_all = fourth(1, c_all)
    bias_grad = jnp.sum(c_all, 0, dtype=f32)
    c_all = reorder(
        c_all.reshape(4, row_count, col_count),
        [dp, dp ^ 1, jnp.where(inner, dp ^ 3, dp ^ 2), jnp.where(inner, dp ^ 2, dp ^ 3)],
    )

    def fifth(k, chain):
        one, two, chain = seq(
            added(g_block(1, sides[k]), b4[k]), added(g_block(3, sides[k]), a4[k]), chain
        )
        a5[k], b5[k] = along(one, PAIRS), along(two, MIDDLE)
        return chain

    a4[0], b4[0], c_all, bias_grad = seq(a4[0], b4[0], c_all, bias_grad)
    c_all = fifth(0, c_all)
    a4[1], b4[1], c_all = seq(a4[1], b4[1], c_all)
    c_all = fifth(1, c_all)

    def gradient(k):
        rows = g_block(0, sides[k]).astype(f32) + a5[k].astype(f32) + b5[k].astype(f32)
        scaled, hat = rows * gain, kept_hat[sides[k]]
        return (
            rows,
            jnp.stack([jnp.sum(scaled, 1), jnp.sum(scaled * hat, 1)]),
            jnp.stack([jnp.sum(rows * hat, 0), jnp.sum(rows, 0)]),
        )

    near1 = jnp.concatenate(b3)
    a5[0], b5[0], near1, c_all = seq(a5[0], b5[0], near1, c_all)
    near3 = [along(near1[:, :half], OUTWARD), None]
    upper, upper_terms, upper_sums = gradient(0)
    a5[1], b5[1], upper_terms, upper_sums = seq(a5[1], b5[1], upper_terms, upper_sums)
    lower, lower_terms, lower_sums = gradient(1)
    row_terms = jnp.concatenate([upper_terms, lower_terms], 1)
    row_terms = row_terms + flip(row_terms, "mp", 1)
    sent, row_terms = seq(near1[:, half:], row_terms)
    near3[1] = along(sent, OUTWARD)
    row_terms = (row_terms + flip(row_terms, "mp", 2)) / full_width
    columns = jnp.stack([stats[2], kept_inv, row_terms[0], row_terms[1]], 1)
    near3[0], columns = seq(near3[0], columns)
    passed, outgoing = boundary(
        upper, lower, kept_rows, columns, gain, summed, bias.reshape(col_count), section
    )
    outgoing = flip(outgoing, "section", 1)
    arrived = lax.all_to_all(outgoing, ("dp", "mp"), split_axis=0, concat_axis=0, tiled=True)

    column_sums, c_all, outgoing = seq(upper_sums + lower_sums, c_all, outgoing)
    column_sums = column_sums + along(column_sums, PAIRS)
    column_grads = column_sums + along(column_sums, [(s, s ^ 2) for s in range(4)])
    width = half // 2
    early = [
        normed_kept,
        jnp.where(inner, jnp.concatenate(a1), jnp.concatenate(a4)),
        jnp.where(inner, jnp.concatenate(b2), jnp.concatenate(a3)),
    ]
    weight_grad = None
    for k in range(4):
        last = near3[k // 2]
        if weight_grad is None:
            last, c_all = seq(last, c_all)
        else:
            last, weight_grad = seq(last, weight_grad)
        cut = lambda value: value[:, k * width:(k + 1) * width]
        own, one, three = (cut(value) for value in early)
        two = jnp.where(inner, cut(near1), last[:, (k % 2) * width:(k % 2 + 1) * width])
        weight_grad = grad_block(
            jnp.concatenate([own, one, two, three]), c_all, weight_grad, k, 4
        )
        if k == 2:
            arrived, column_grads, weight_grad = seq(arrived, column_grads, weight_grad)
    next_in = joined(arrived, section)

    return (
        next_in.reshape(fwd_in.shape),
        passed.reshape(fwd_in.shape),
        weight_grad.reshape(weight.shape),
        bias_grad.reshape(1, col_count),
        column_grads.reshape(1, 2, col_count),
    )


def shards(*arrays):
    if lax.axis_size("dp") == 4 and lax.axis_size("mp") == 4:
        return shards_of_four(*arrays)
    return shards_of_any_size(*arrays)


def solution(mesh):
    placed = (
        P("section", "dp", "mp", None, None),
        P("section", "dp", "mp", None, None),
        P("section", "dp", "mp", None, None),
        P("section", "mp", "dp"),
        P("section", "dp"),
        P("section", "mp"),
        P("section", "mp"),
    )
    return jax.shard_map(
        shards,
        mesh=mesh,
        in_specs=placed,
        out_specs=(
            P("section", "dp", "mp", None, None),
            P("section", "dp", "mp", None, None),
            P("section", "mp", "dp"),
            P("section", "dp"),
            P("section", None, "mp"),
        ),
        check_vma=False,
    )
```

```python
import functools

import jax
import jax.numpy as jnp
from jax import lax
from jax.experimental import pallas as pl
from jax.experimental.pallas import tpu as pltpu
from jax.sharding import PartitionSpec as P

eps = 1e-05
LIGHT = pl.CostEstimate(flops=1, bytes_accessed=1, transcendentals=0)


def flip(value, axis, mask):
    n = lax.axis_size(axis)
    return lax.ppermute(value, axis, [(s, s ^ mask) for s in range(n)])


def grad_kernel(v_ref, c_ref, *rest):
    out_ref, turned = rest[-2:]

    @pl.when(pl.program_id(0) == 0)
    def _():
        turned[...] = v_ref[...].T

    out_ref[...] = jnp.dot(turned[...], c_ref[...], preferred_element_type=jnp.float32)


def grad_block(kept_block, upstream, filled, block, blocks):
    tokens, width = kept_block.shape
    cols = upstream.shape[1]
    step = 768
    specs = [
        pl.BlockSpec((tokens, width), lambda j: (0, 0)),
        pl.BlockSpec((tokens, step), lambda j: (0, j)),
    ]
    operands = [kept_block, upstream]
    aliases = {}
    if filled is not None:
        specs.append(pl.BlockSpec(memory_space=pl.ANY))
        operands.append(filled)
        aliases = {2: 0}
    return pl.pallas_call(
        grad_kernel,
        grid=(cols // step,),
        in_specs=specs,
        out_specs=pl.BlockSpec((width, step), lambda j: (block, j)),
        out_shape=jax.ShapeDtypeStruct((width * blocks, cols), jnp.float32),
        scratch_shapes=[pltpu.VMEM((width, tokens), jnp.bfloat16)],
        input_output_aliases=aliases,
        compiler_params=pltpu.CompilerParams(vmem_limit_bytes=32 * 2**20),
        cost_estimate=LIGHT,
    )(*operands)


def share_kernel(count, turned, *refs):
    w_ref, out_ref = refs[2 * count], refs[-1]
    half = refs[0].shape[1]
    for k in range(count):
        total = None
        for side in range(2):
            cut = pl.ds(side * half, half)
            part = lax.dot_general(
                refs[2 * k + side][...],
                w_ref[:, cut] if turned else w_ref[cut, :],
                (((1,), (1 if turned else 0,)), ((), ())),
                preferred_element_type=jnp.float32,
            )
            total = part if total is None else total + part
        out_ref[k] = total.astype(jnp.bfloat16)


def shares(blocks, w, turned, filled, place, total, total_rows):
    count = len(blocks)
    halves = []
    for block in blocks:
        halves += list(block) if isinstance(block, tuple) else [(block, 0, 0), (block, 1, 0)]
    rows = total_rows // total
    depth = w.shape[1] if turned else w.shape[0]
    cols = w.shape[0] if turned else w.shape[1]
    step = 512
    specs = [
        pl.BlockSpec((rows, depth // 2), functools.partial(lambda side, at, j: (at, side), side, at))
        for array, side, at in halves
    ]
    if turned:
        specs.append(pl.BlockSpec((step, depth), lambda j: (j, 0)))
    else:
        specs.append(pl.BlockSpec((depth, step), lambda j: (0, j)))
    operands = [array for array, side, at in halves] + [w]
    aliases = {}
    if filled is not None:
        specs.append(pl.BlockSpec(memory_space=pl.ANY))
        operands.append(filled)
        aliases = {2 * count + 1: 0}
    return pl.pallas_call(
        functools.partial(share_kernel, count, turned),
        grid=(cols // step,),
        in_specs=specs,
        out_specs=pl.BlockSpec((count, rows, step), lambda j: (place // count, 0, j)),
        out_shape=jax.ShapeDtypeStruct((total, rows, cols), jnp.bfloat16),
        input_output_aliases=aliases,
        compiler_params=pltpu.CompilerParams(vmem_limit_bytes=32 * 2**20),
        cost_estimate=LIGHT,
    )(*operands)


def normed_kernel(rows_ref, stats_ref, gain_ref, shift_ref, out_ref):
    stats = stats_ref[...]
    hat = (rows_ref[...].astype(jnp.float32) - stats[:, 0:1]) * stats[:, 1:2]
    out_ref[...] = (hat * gain_ref[...] + shift_ref[...]).astype(jnp.bfloat16)


def normed(rows, row_stats, gain, shift):
    mean, square_mean = row_stats[0], row_stats[1]
    stats = jnp.stack([mean, lax.rsqrt(square_mean - mean * mean + eps)], 1)
    count, cols = rows.shape
    part = 64
    line = pl.BlockSpec((1, cols), lambda j: (0, 0))
    wide = pl.BlockSpec((part, cols), lambda j: (j, 0))
    return pl.pallas_call(
        normed_kernel,
        grid=(count // part,),
        in_specs=[wide, pl.BlockSpec((part, 2), lambda j: (j, 0)), line, line],
        out_specs=wide,
        out_shape=jax.ShapeDtypeStruct((count, cols), jnp.bfloat16),
        compiler_params=pltpu.CompilerParams(vmem_limit_bytes=32 * 2**20),
        cost_estimate=LIGHT,
    )(rows, stats, gain.reshape(1, cols), shift.reshape(1, cols))


def reorder_kernel(order_ref, stack_ref, out_ref):
    out_ref[...] = stack_ref[...]


def reorder(stack, order):
    count, rows, cols = stack.shape
    out = pl.pallas_call(
        reorder_kernel,
        grid_spec=pltpu.PrefetchScalarGridSpec(
            num_scalar_prefetch=1,
            grid=(count,),
            in_specs=[pl.BlockSpec((1, rows, cols), lambda j, order: (order[j], 0, 0))],
            out_specs=pl.BlockSpec((1, rows, cols), lambda j, order: (j, 0, 0)),
        ),
        out_shape=jax.ShapeDtypeStruct(stack.shape, stack.dtype),
        compiler_params=pltpu.CompilerParams(vmem_limit_bytes=32 * 2**20),
        cost_estimate=LIGHT,
    )(jnp.stack(order).astype(jnp.int32), stack)
    return out.reshape(count * rows, cols)


def boundary_kernel(g_ref, kept_ref, columns_ref, gain_ref, h_ref, bias_ref, section_ref, passed_ref, out_ref):
    step = pl.program_id(0)
    first = section_ref[0] == 0
    groups = pl.num_programs(0)
    width = out_ref.shape[2]
    f32 = jnp.float32
    columns = columns_ref[...]
    mean, inverse, one, two = (columns[:, k:k + 1] for k in range(4))
    for f in range(out_ref.shape[0] // 4):
        cut = pl.ds(f * width, width)
        hat = (kept_ref[:, cut].astype(f32) - mean) * inverse
        grad = (inverse * (g_ref[:, cut] * gain_ref[:, cut] - one - hat * two)).astype(jnp.bfloat16)
        output = (h_ref[:, cut].astype(f32) + bias_ref[:, cut]).astype(jnp.bfloat16)
        passed_ref[:, cut] = jnp.where(first, grad, output)
        out_ref[jnp.where(first, step * groups + f, f * groups + step)] = jnp.where(
            first, output, grad
        )


def boundary(grad_rows, kept_rows, columns, gain, summed, bias, section):
    rows, cols = kept_rows.shape
    part = rows // 4
    wide = pl.BlockSpec((part, cols), lambda j: (j, 0))
    line = pl.BlockSpec((1, cols), lambda j: (0, 0))
    return pl.pallas_call(
        boundary_kernel,
        grid=(4,),
        in_specs=[
            wide, wide, pl.BlockSpec((part, 4), lambda j: (j, 0)), line, wide, line,
            pl.BlockSpec(memory_space=pltpu.SMEM),
        ],
        out_specs=[wide, pl.BlockSpec((16, part, cols // 4), lambda j: (0, 0, 0))],
        out_shape=[
            jax.ShapeDtypeStruct((rows, cols), jnp.bfloat16),
            jax.ShapeDtypeStruct((16, part, cols // 4), jnp.bfloat16),
        ],
        compiler_params=pltpu.CompilerParams(vmem_limit_bytes=32 * 2**20),
        cost_estimate=LIGHT,
    )(
        grad_rows, kept_rows, columns, gain.reshape(1, cols), summed, bias.reshape(1, cols),
        section.reshape(1),
    )


def joined_kernel(pieces_ref, section_ref, out_ref):
    step = pl.program_id(0)
    width = pieces_ref.shape[2]
    for c in range(4):
        piece = jnp.where(section_ref[0] == 0, step * 4 + c, c * 4 + step)
        out_ref[:, pl.ds(c * width, width)] = pieces_ref[piece]


def joined(pieces, section):
    count, part, width = pieces.shape
    return pl.pallas_call(
        joined_kernel,
        grid=(4,),
        in_specs=[
            pl.BlockSpec((count, part, width), lambda j: (0, 0, 0)),
            pl.BlockSpec(memory_space=pltpu.SMEM),
        ],
        out_specs=pl.BlockSpec((part, 4 * width), lambda j: (j, 0)),
        out_shape=jax.ShapeDtypeStruct((4 * part, 4 * width), pieces.dtype),
        compiler_params=pltpu.CompilerParams(vmem_limit_bytes=32 * 2**20),
        cost_estimate=LIGHT,
    )(pieces, section.reshape(1))


def from_partner(value, axis, stride):
    mask = 2**stride
    pairs = [(source, source ^ mask) for source in range(lax.axis_size(axis))]
    return lax.ppermute(value, axis, pairs)


def standardize(values, totals, squares, full_width):
    mean_val = totals / full_width
    spread = squares / full_width - mean_val * mean_val
    inv_std = lax.rsqrt(spread + eps)
    return ((values - mean_val[:, None]) * inv_std[:, None], inv_std)


def regroup(outgoing, groups):
    flat_buffer = outgoing.reshape((groups * groups,) + outgoing.shape[2:])
    moved_data = lax.all_to_all(flat_buffer, ("dp", "mp"), split_axis=0, concat_axis=0, tiled=True)
    return moved_data.reshape(outgoing.shape)


def shards_of_any_size(fwd_in, kept_in, cotangent, weight, bias, norm_gain, norm_shift):
    section_index = lax.axis_index("section")
    groups = lax.axis_size("dp")
    row_count = fwd_in.shape[3]
    col_count = fwd_in.shape[4]
    full_width = col_count * lax.axis_size("mp")
    piece_rows = row_count // groups
    piece_cols = col_count // groups
    weight_tile = weight.reshape(col_count, col_count)
    gain_cols = norm_gain.reshape(col_count)
    shift_cols = norm_shift.reshape(col_count)
    fresh_rows = fwd_in.reshape(row_count, col_count).astype(jnp.float32)
    kept_values = kept_in.reshape(row_count, col_count).astype(jnp.float32)
    upstream = cotangent.reshape(row_count, col_count)
    row_stats = lax.psum(
        (
            jnp.sum(fresh_rows, 1),
            jnp.sum(fresh_rows * fresh_rows, 1),
            jnp.sum(kept_values, 1),
            jnp.sum(kept_values * kept_values, 1),
        ),
        "mp",
    )
    fresh_hat, unused_scale = standardize(fresh_rows, row_stats[0], row_stats[1], full_width)
    kept_hat, kept_inv = standardize(kept_values, row_stats[2], row_stats[3], full_width)
    normed = (fresh_hat * gain_cols + shift_cols).astype(jnp.bfloat16)
    normed_kept = (kept_hat * gain_cols + shift_cols).astype(jnp.bfloat16)
    upstream_all = lax.all_gather(upstream, "mp", axis=0, tiled=True)
    gathered, gathered_kept = (
        lax.all_gather(normed, "dp", axis=0, tiled=True),
        lax.all_gather(normed_kept, "dp", axis=0, tiled=True),
    )
    weight_grad = lax.dot_general(
        gathered_kept, upstream_all, (((0,), (0,)), ((), ())), preferred_element_type=jnp.float32
    )
    segment = gathered
    summed = lax.psum_scatter(
        jnp.dot(segment, weight_tile, preferred_element_type=jnp.float32).astype(jnp.bfloat16),
        "mp",
        scatter_dimension=0,
        tiled=True,
    ).astype(jnp.float32)
    output = (summed + bias.reshape(col_count)).astype(jnp.bfloat16)
    bias_grad = jnp.sum(upstream_all, 0, dtype=jnp.float32)
    segment = upstream_all
    grad_rows = lax.psum_scatter(
        lax.dot_general(
            segment, weight_tile, (((1,), (1,)), ((), ())), preferred_element_type=jnp.float32
        ).astype(jnp.bfloat16),
        "dp",
        scatter_dimension=0,
        tiled=True,
    ).astype(jnp.float32)
    scaled = grad_rows * gain_cols
    column_grads = lax.psum((jnp.sum(grad_rows * kept_hat, 0), jnp.sum(grad_rows, 0)), "dp")
    row_terms = lax.psum((jnp.sum(scaled, 1), jnp.sum(scaled * kept_hat, 1)), "mp")
    input_grad = (
        kept_inv[:, None]
        * (
            scaled
            - row_terms[0][:, None] / full_width
            - kept_hat * (row_terms[1][:, None] / full_width)
        )
    ).astype(jnp.bfloat16)
    out_pack = output.reshape(groups, piece_rows, groups, piece_cols).transpose(0, 2, 1, 3)
    grad_pack = input_grad.reshape(groups, piece_rows, groups, piece_cols).transpose(2, 0, 1, 3)
    outgoing = jnp.where(section_index == 0, out_pack, grad_pack)
    arrived = from_partner(regroup(outgoing, groups), "section", 0)
    as_cotangent = arrived.transpose(0, 2, 1, 3).reshape(row_count, col_count)
    as_input = arrived.transpose(1, 2, 0, 3).reshape(row_count, col_count)
    next_in = jnp.where(section_index == 0, as_cotangent, as_input)
    passed = jnp.where(section_index == 0, input_grad, output)
    return (
        next_in.reshape(fwd_in.shape),
        passed.reshape(fwd_in.shape),
        weight_grad.reshape(1, col_count, col_count),
        bias_grad.reshape(1, col_count),
        jnp.stack([column_grads[0], column_grads[1]]).reshape(1, 2, col_count),
    )


PAIRS = [(0, 1), (1, 0), (2, 3), (3, 2)]
MIDDLE = [(1, 2), (2, 1)]
INWARD = [(0, 1), (3, 2)]
OUTWARD = [(1, 0), (2, 3)]


def shards_of_four(fwd_in, kept_in, cotangent, weight, bias, norm_gain, norm_shift):
    f32, bf16 = jnp.float32, jnp.bfloat16
    section = lax.axis_index("section")
    dp, mp = lax.axis_index("dp"), lax.axis_index("mp")
    inner = (dp == 1) | (dp == 2)
    row_count, col_count = fwd_in.shape[3], fwd_in.shape[4]
    full_width = col_count * 4
    half = col_count // 2
    w = weight.reshape(weight.shape[1], weight.shape[2])
    gain = norm_gain.reshape(col_count)
    shift = norm_shift.reshape(col_count)
    fresh_rows = fwd_in.reshape(row_count, col_count)
    kept_rows = kept_in.reshape(row_count, col_count)
    upstream = cotangent.reshape(row_count, col_count)
    along = lambda value, pairs: lax.ppermute(value, "dp", pairs)
    pick = lambda stack, k: lax.dynamic_index_in_dim(stack, k, 0, keepdims=False)

    def standardize(values, mean, square_mean):
        inverse = lax.rsqrt(square_mean - mean * mean + eps)
        return (values.astype(f32) - mean[:, None]) * inverse[:, None], inverse

    def added(one, two):
        return (one.astype(f32) + two.astype(f32)).astype(bf16)

    seq = lambda *values: lax.optimization_barrier(values)
    either = lambda from_inner, from_outer: jnp.where(inner, from_inner, from_outer)

    c_all = lax.all_gather(upstream, "mp", axis=0, tiled=True)
    u1a, u1b = along(fresh_rows, PAIRS), along(fresh_rows, MIDDLE)
    fresh, kept = fresh_rows.astype(f32), kept_rows.astype(f32)
    sums = jnp.stack(
        [jnp.sum(fresh, 1), jnp.sum(fresh * fresh, 1), jnp.sum(kept, 1), jnp.sum(kept * kept, 1)]
    )
    sums = sums + flip(sums, "mp", 1)
    stats = (sums + flip(sums, "mp", 2)) / full_width
    kept_hat, kept_inv = standardize(kept_rows, stats[2], stats[3])
    normed_kept = normed(kept_rows, stats[2:], gain, shift)
    pair_stats = jnp.stack([stats[:2], along(stats[:2], PAIRS)])
    u1a, u1b, normed_kept, pair_stats = seq(u1a, u1b, normed_kept, pair_stats)

    a1, b1 = along(either(u1b, normed_kept), PAIRS), along(u1a, MIDDLE)
    h_stack = shares(
        [normed(fresh_rows, stats, gain, shift), normed(u1a, pair_stats[1], gain, shift)],
        w, False, None, 0, 4, 4 * row_count,
    )
    a1, b1, h_stack, c_all, pair_stats = seq(a1, b1, h_stack, c_all, pair_stats)

    a2, b2 = along(b1, OUTWARD), along(a1, MIDDLE)
    all_stats = jnp.concatenate([pair_stats, along(pair_stats, [(s, s ^ 2) for s in range(4)])])
    g_stack = None
    for first in (0, 2):
        blocks = [((c_all, 0, b), (c_all, 1, b)) for b in (first, first + 1)]
        g_stack = shares(blocks, w, True, g_stack, first, 4, 4 * row_count)
    a2, b2, g_stack, all_stats, normed_kept = seq(a2, b2, g_stack, all_stats, normed_kept)
    g_block = lambda k: pick(g_stack, dp ^ k)

    a3, b3 = along(either(b2, g_block(3)), PAIRS), along(normed_kept, MIDDLE)
    two, three = jnp.where(inner, 3, 2), jnp.where(inner, 2, 3)
    h_stack = shares(
        [
            normed(either(u1b, a1), pick(all_stats, two), gain, shift),
            normed(either(b1, a2), pick(all_stats, three), gain, shift),
        ],
        w, False, h_stack, 2, 4, 4 * row_count,
    )
    a3, b3, h_stack = seq(a3, b3, h_stack)

    x2 = added(g_block(2), jnp.where(inner, a3, jnp.zeros_like(a3)))
    a4, b4 = along(either(normed_kept, x2), PAIRS), along(x2, MIDDLE)
    places = [dp ^ b for b in range(4)]
    places = [jnp.where(inner & (at >= 2), at ^ 1, at) for at in places]
    h_all = reorder(h_stack, places)
    summed = lax.psum_scatter(h_all, "mp", scatter_dimension=0, tiled=True)
    bias_grad = jnp.sum(c_all, 0, dtype=f32)
    c_all = reorder(c_all.reshape(4, row_count, col_count), [dp, dp ^ 1, dp ^ two, dp ^ three])
    a4, b4, c_all, bias_grad = seq(a4, b4, c_all, bias_grad)

    a5 = along(added(g_block(1), b4), PAIRS)
    b5 = along(added(g_block(3), a4), MIDDLE)
    near3 = [along(b3[:, :half], OUTWARD), None]
    a5, b5, near3[0], b3 = seq(a5, b5, near3[0], b3)

    near3[1] = along(b3[:, half:], OUTWARD)
    grad_rows = g_block(0).astype(f32) + a5.astype(f32) + b5.astype(f32)
    scaled = grad_rows * gain
    row_terms = jnp.stack([jnp.sum(scaled, 1), jnp.sum(scaled * kept_hat, 1)])
    column_sums = jnp.stack([jnp.sum(grad_rows * kept_hat, 0), jnp.sum(grad_rows, 0)])
    row_terms = row_terms + flip(row_terms, "mp", 1)
    row_terms = (row_terms + flip(row_terms, "mp", 2)) / full_width
    columns = jnp.stack([stats[2], kept_inv, row_terms[0], row_terms[1]], 1)
    near3[1], columns = seq(near3[1], columns)
    passed, outgoing = boundary(
        grad_rows, kept_rows, columns, gain, summed, bias.reshape(col_count), section
    )
    arrived = lax.all_to_all(outgoing, ("dp", "mp"), split_axis=0, concat_axis=0, tiled=True)

    c_all, outgoing, near3[0], normed_kept = seq(c_all, outgoing, near3[0], normed_kept)
    early = [normed_kept, either(a1, a4), either(b2, a3)]
    weight_grad = None
    for k in range(2):
        cut = lambda value: value[:, k * half:(k + 1) * half]
        own, one, three = (cut(value) for value in early)
        kept_all = jnp.concatenate([own, one, either(cut(b3), near3[k]), three])
        if weight_grad is not None:
            kept_all, weight_grad = seq(kept_all, weight_grad)
        weight_grad = grad_block(kept_all, c_all, weight_grad, k, 2)
        if k == 0:
            column_sums, weight_grad = seq(column_sums, weight_grad)
            column_sums = column_sums + along(column_sums, PAIRS)
            column_grads = column_sums + along(column_sums, [(s, s ^ 2) for s in range(4)])
    arrived, column_grads, weight_grad = seq(arrived, column_grads, weight_grad)
    next_in = joined(flip(arrived, "section", 1), section)

    return (
        next_in.reshape(fwd_in.shape),
        passed.reshape(fwd_in.shape),
        weight_grad.reshape(weight.shape),
        bias_grad.reshape(1, col_count),
        column_grads.reshape(1, 2, col_count),
    )


def shards(*arrays):
    if lax.axis_size("dp") == 4 and lax.axis_size("mp") == 4:
        return shards_of_four(*arrays)
    return shards_of_any_size(*arrays)


def solution(mesh):
    placed = (
        P("section", "dp", "mp", None, None),
        P("section", "dp", "mp", None, None),
        P("section", "dp", "mp", None, None),
        P("section", "mp", "dp"),
        P("section", "dp"),
        P("section", "mp"),
        P("section", "mp"),
    )
    return jax.shard_map(
        shards,
        mesh=mesh,
        in_specs=placed,
        out_specs=(
            P("section", "dp", "mp", None, None),
            P("section", "dp", "mp", None, None),
            P("section", "mp", "dp"),
            P("section", "dp"),
            P("section", None, "mp"),
        ),
        check_vma=False,
    )
```

```python
import functools

import jax
import jax.numpy as jnp
from jax import lax
from jax.experimental import pallas as pl
from jax.experimental.pallas import tpu as pltpu
from jax.sharding import PartitionSpec as P

eps = 1e-05
GRANT = 56 * 2**20
LIGHT = pl.CostEstimate(flops=1, bytes_accessed=1, transcendentals=0)


def flip(value, axis, mask):
    n = lax.axis_size(axis)
    return lax.ppermute(value, axis, [(s, s ^ mask) for s in range(n)])


def grad_kernel(v_ref, c_ref, *rest):
    out_ref, turned = rest[-2:]

    @pl.when(pl.program_id(0) == 0)
    def _():
        turned[...] = v_ref[...].T

    out_ref[...] = jnp.dot(turned[...], c_ref[...], preferred_element_type=jnp.float32)


def grad_block(kept_block, upstream, filled, block, blocks):
    tokens, width = kept_block.shape
    cols = upstream.shape[1]
    step = 768
    specs = [
        pl.BlockSpec((tokens, width), lambda j: (0, 0)),
        pl.BlockSpec((tokens, step), lambda j: (0, j)),
    ]
    operands = [kept_block, upstream]
    aliases = {}
    if filled is not None:
        specs.append(pl.BlockSpec(memory_space=pl.ANY))
        operands.append(filled)
        aliases = {2: 0}
    return pl.pallas_call(
        grad_kernel,
        grid=(cols // step,),
        in_specs=specs,
        out_specs=pl.BlockSpec((width, step), lambda j: (block, j)),
        out_shape=jax.ShapeDtypeStruct((width * blocks, cols), jnp.float32),
        scratch_shapes=[pltpu.VMEM((width, tokens), jnp.bfloat16)],
        input_output_aliases=aliases,
        compiler_params=pltpu.CompilerParams(vmem_limit_bytes=GRANT),
        cost_estimate=LIGHT,
    )(*operands)


def share_kernel(count, turned, *refs):
    w_ref, out_ref = refs[2 * count], refs[-1]
    half = refs[0].shape[1]
    for k in range(count):
        total = None
        for side in range(2):
            cut = pl.ds(side * half, half)
            part = lax.dot_general(
                refs[2 * k + side][...],
                w_ref[:, cut] if turned else w_ref[cut, :],
                (((1,), (1 if turned else 0,)), ((), ())),
                preferred_element_type=jnp.float32,
            )
            total = part if total is None else total + part
        out_ref[k] = total.astype(jnp.bfloat16)


def shares(blocks, w, turned, filled, place, total, total_rows):
    count = len(blocks)
    halves = []
    for block in blocks:
        halves += list(block) if isinstance(block, tuple) else [(block, 0, 0), (block, 1, 0)]
    rows = total_rows // total
    depth = w.shape[1] if turned else w.shape[0]
    cols = w.shape[0] if turned else w.shape[1]
    step = 512
    specs = [
        pl.BlockSpec((rows, depth // 2), functools.partial(lambda side, at, j: (at, side), side, at))
        for array, side, at in halves
    ]
    if turned:
        specs.append(pl.BlockSpec((step, depth), lambda j: (j, 0)))
    else:
        specs.append(pl.BlockSpec((depth, step), lambda j: (0, j)))
    operands = [array for array, side, at in halves] + [w]
    aliases = {}
    if filled is not None:
        specs.append(pl.BlockSpec(memory_space=pl.ANY))
        operands.append(filled)
        aliases = {2 * count + 1: 0}
    return pl.pallas_call(
        functools.partial(share_kernel, count, turned),
        grid=(cols // step,),
        in_specs=specs,
        out_specs=pl.BlockSpec((count, rows, step), lambda j: (place // count, 0, j)),
        out_shape=jax.ShapeDtypeStruct((total, rows, cols), jnp.bfloat16),
        input_output_aliases=aliases,
        compiler_params=pltpu.CompilerParams(vmem_limit_bytes=GRANT),
        cost_estimate=LIGHT,
    )(*operands)


def normed_kernel(rows_ref, stats_ref, gain_ref, shift_ref, out_ref):
    stats = stats_ref[...]
    hat = (rows_ref[...].astype(jnp.float32) - stats[:, 0:1]) * stats[:, 1:2]
    out_ref[...] = (hat * gain_ref[...] + shift_ref[...]).astype(jnp.bfloat16)


def normed(rows, row_stats, gain, shift):
    mean, square_mean = row_stats[0], row_stats[1]
    stats = jnp.stack([mean, lax.rsqrt(square_mean - mean * mean + eps)], 1)
    count, cols = rows.shape
    part = 64
    line = pl.BlockSpec((1, cols), lambda j: (0, 0))
    wide = pl.BlockSpec((part, cols), lambda j: (j, 0))
    return pl.pallas_call(
        normed_kernel,
        grid=(count // part,),
        in_specs=[wide, pl.BlockSpec((part, 2), lambda j: (j, 0)), line, line],
        out_specs=wide,
        out_shape=jax.ShapeDtypeStruct((count, cols), jnp.bfloat16),
        compiler_params=pltpu.CompilerParams(vmem_limit_bytes=GRANT),
        cost_estimate=LIGHT,
    )(rows, stats, gain.reshape(1, cols), shift.reshape(1, cols))


def reorder_kernel(order_ref, stack_ref, out_ref):
    out_ref[...] = stack_ref[...]


def reorder(stack, order):
    count, rows, cols = stack.shape
    out = pl.pallas_call(
        reorder_kernel,
        grid_spec=pltpu.PrefetchScalarGridSpec(
            num_scalar_prefetch=1,
            grid=(count,),
            in_specs=[pl.BlockSpec((1, rows, cols), lambda j, order: (order[j], 0, 0))],
            out_specs=pl.BlockSpec((1, rows, cols), lambda j, order: (j, 0, 0)),
        ),
        out_shape=jax.ShapeDtypeStruct(stack.shape, stack.dtype),
        compiler_params=pltpu.CompilerParams(vmem_limit_bytes=GRANT),
        cost_estimate=LIGHT,
    )(jnp.stack(order).astype(jnp.int32), stack)
    return out.reshape(count * rows, cols)


def turn_kernel(at_ref, share_ref, arrived_ref, kept_ref, sent_ref, sum_ref):
    inner = at_ref[1] == 1
    f32 = jnp.float32
    arrived = arrived_ref[...].astype(f32)
    total = share_ref[0].astype(f32) + jnp.where(inner, arrived, jnp.zeros_like(arrived))
    total = total.astype(jnp.bfloat16)
    sum_ref[...] = total
    sent_ref[...] = jnp.where(inner, kept_ref[...], total)


def turn(stack, at, arrived, kept, inner):
    count, rows, cols = stack.shape
    part = 64
    wide = pl.BlockSpec((part, cols), lambda j, at: (j, 0))
    return pl.pallas_call(
        turn_kernel,
        grid_spec=pltpu.PrefetchScalarGridSpec(
            num_scalar_prefetch=1,
            grid=(rows // part,),
            in_specs=[pl.BlockSpec((1, part, cols), lambda j, at: (at[0], j, 0)), wide, wide],
            out_specs=[wide, wide],
        ),
        out_shape=[jax.ShapeDtypeStruct((rows, cols), stack.dtype)] * 2,
        compiler_params=pltpu.CompilerParams(vmem_limit_bytes=GRANT),
        cost_estimate=LIGHT,
    )(jnp.stack([at, inner.astype(jnp.int32)]).astype(jnp.int32), stack, arrived, kept)


def joint_sums_kernel(at_ref, one_ref, two_ref, first_ref, second_ref, out_one, out_two):
    f32, bf16 = jnp.float32, jnp.bfloat16
    out_one[...] = (one_ref[0].astype(f32) + first_ref[...].astype(f32)).astype(bf16)
    out_two[...] = (two_ref[0].astype(f32) + second_ref[...].astype(f32)).astype(bf16)


def joint_sums(stack, at_one, at_two, first, second):
    count, rows, cols = stack.shape
    part = 64
    wide = pl.BlockSpec((part, cols), lambda j, at: (j, 0))
    return pl.pallas_call(
        joint_sums_kernel,
        grid_spec=pltpu.PrefetchScalarGridSpec(
            num_scalar_prefetch=1,
            grid=(rows // part,),
            in_specs=[
                pl.BlockSpec((1, part, cols), lambda j, at: (at[0], j, 0)),
                pl.BlockSpec((1, part, cols), lambda j, at: (at[1], j, 0)),
                wide,
                wide,
            ],
            out_specs=[wide, wide],
        ),
        out_shape=[jax.ShapeDtypeStruct((rows, cols), stack.dtype)] * 2,
        compiler_params=pltpu.CompilerParams(vmem_limit_bytes=GRANT),
        cost_estimate=LIGHT,
    )(jnp.stack([at_one, at_two]).astype(jnp.int32), stack, stack, first, second)


def gradient_kernel(at_ref, share_ref, a_ref, b_ref, kept_ref, stats_ref, gain_ref, rows_ref, terms_ref, sums_ref):
    f32 = jnp.float32
    stats = stats_ref[...]
    rows = share_ref[0].astype(f32) + a_ref[...].astype(f32) + b_ref[...].astype(f32)
    hat = (kept_ref[...].astype(f32) - stats[:, 0:1]) * stats[:, 1:2]
    rows_ref[...] = rows
    scaled = rows * gain_ref[...]
    terms_ref[:, 0:1] = jnp.sum(scaled, 1, keepdims=True)
    terms_ref[:, 1:2] = jnp.sum(scaled * hat, 1, keepdims=True)

    @pl.when(pl.program_id(0) == 0)
    def _():
        sums_ref[...] = jnp.zeros_like(sums_ref)

    sums_ref[0:1, :] += jnp.sum(rows * hat, 0, keepdims=True)
    sums_ref[1:2, :] += jnp.sum(rows, 0, keepdims=True)


def gradient(stack, at, a, b, kept_rows, stats, gain):
    count, rows, cols = stack.shape
    part = 64
    wide = pl.BlockSpec((part, cols), lambda j, at: (j, 0))
    narrow = pl.BlockSpec((part, 2), lambda j, at: (j, 0))
    return pl.pallas_call(
        gradient_kernel,
        grid_spec=pltpu.PrefetchScalarGridSpec(
            num_scalar_prefetch=1,
            grid=(rows // part,),
            in_specs=[
                pl.BlockSpec((1, part, cols), lambda j, at: (at[0], j, 0)),
                wide, wide, wide, narrow,
                pl.BlockSpec((1, cols), lambda j, at: (0, 0)),
            ],
            out_specs=[wide, narrow, pl.BlockSpec((2, cols), lambda j, at: (0, 0))],
        ),
        out_shape=[
            jax.ShapeDtypeStruct((rows, cols), jnp.float32),
            jax.ShapeDtypeStruct((rows, 2), jnp.float32),
            jax.ShapeDtypeStruct((2, cols), jnp.float32),
        ],
        compiler_params=pltpu.CompilerParams(vmem_limit_bytes=GRANT),
        cost_estimate=LIGHT,
    )(at.reshape(1).astype(jnp.int32), stack, a, b, kept_rows, stats, gain.reshape(1, cols))


def boundary_kernel(g_ref, kept_ref, columns_ref, gain_ref, h_ref, bias_ref, section_ref, passed_ref, out_ref):
    step = pl.program_id(0)
    first = section_ref[0] == 0
    groups = pl.num_programs(0)
    width = out_ref.shape[2]
    f32 = jnp.float32
    columns = columns_ref[...]
    mean, inverse, one, two = (columns[:, k:k + 1] for k in range(4))
    for f in range(out_ref.shape[0] // 4):
        cut = pl.ds(f * width, width)
        hat = (kept_ref[:, cut].astype(f32) - mean) * inverse
        grad = (inverse * (g_ref[:, cut] * gain_ref[:, cut] - one - hat * two)).astype(jnp.bfloat16)
        output = (h_ref[:, cut].astype(f32) + bias_ref[:, cut]).astype(jnp.bfloat16)
        passed_ref[:, cut] = jnp.where(first, grad, output)
        out_ref[jnp.where(first, step * groups + f, f * groups + step)] = jnp.where(
            first, output, grad
        )


def boundary(grad_rows, kept_rows, columns, gain, summed, bias, section):
    rows, cols = kept_rows.shape
    part = rows // 4
    wide = pl.BlockSpec((part, cols), lambda j: (j, 0))
    line = pl.BlockSpec((1, cols), lambda j: (0, 0))
    return pl.pallas_call(
        boundary_kernel,
        grid=(4,),
        in_specs=[
            wide, wide, pl.BlockSpec((part, 4), lambda j: (j, 0)), line, wide, line,
            pl.BlockSpec(memory_space=pltpu.SMEM),
        ],
        out_specs=[wide, pl.BlockSpec((16, part, cols // 4), lambda j: (0, 0, 0))],
        out_shape=[
            jax.ShapeDtypeStruct((rows, cols), jnp.bfloat16),
            jax.ShapeDtypeStruct((16, part, cols // 4), jnp.bfloat16),
        ],
        compiler_params=pltpu.CompilerParams(vmem_limit_bytes=GRANT),
        cost_estimate=LIGHT,
    )(
        grad_rows, kept_rows, columns, gain.reshape(1, cols), summed, bias.reshape(1, cols),
        section.reshape(1),
    )


def joined_kernel(pieces_ref, section_ref, out_ref):
    step = pl.program_id(0)
    width = pieces_ref.shape[2]
    for c in range(4):
        piece = jnp.where(section_ref[0] == 0, step * 4 + c, c * 4 + step)
        out_ref[:, pl.ds(c * width, width)] = pieces_ref[piece]


def joined(pieces, section):
    count, part, width = pieces.shape
    return pl.pallas_call(
        joined_kernel,
        grid=(4,),
        in_specs=[
            pl.BlockSpec((count, part, width), lambda j: (0, 0, 0)),
            pl.BlockSpec(memory_space=pltpu.SMEM),
        ],
        out_specs=pl.BlockSpec((part, 4 * width), lambda j: (j, 0)),
        out_shape=jax.ShapeDtypeStruct((4 * part, 4 * width), pieces.dtype),
        compiler_params=pltpu.CompilerParams(vmem_limit_bytes=GRANT),
        cost_estimate=LIGHT,
    )(pieces, section.reshape(1))


def from_partner(value, axis, stride):
    mask = 2**stride
    pairs = [(source, source ^ mask) for source in range(lax.axis_size(axis))]
    return lax.ppermute(value, axis, pairs)


def standardize(values, totals, squares, full_width):
    mean_val = totals / full_width
    spread = squares / full_width - mean_val * mean_val
    inv_std = lax.rsqrt(spread + eps)
    return ((values - mean_val[:, None]) * inv_std[:, None], inv_std)


def regroup(outgoing, groups):
    flat_buffer = outgoing.reshape((groups * groups,) + outgoing.shape[2:])
    moved_data = lax.all_to_all(flat_buffer, ("dp", "mp"), split_axis=0, concat_axis=0, tiled=True)
    return moved_data.reshape(outgoing.shape)


def shards_of_any_size(fwd_in, kept_in, cotangent, weight, bias, norm_gain, norm_shift):
    section_index = lax.axis_index("section")
    groups = lax.axis_size("dp")
    row_count = fwd_in.shape[3]
    col_count = fwd_in.shape[4]
    full_width = col_count * lax.axis_size("mp")
    piece_rows = row_count // groups
    piece_cols = col_count // groups
    weight_tile = weight.reshape(col_count, col_count)
    gain_cols = norm_gain.reshape(col_count)
    shift_cols = norm_shift.reshape(col_count)
    fresh_rows = fwd_in.reshape(row_count, col_count).astype(jnp.float32)
    kept_values = kept_in.reshape(row_count, col_count).astype(jnp.float32)
    upstream = cotangent.reshape(row_count, col_count)
    row_stats = lax.psum(
        (
            jnp.sum(fresh_rows, 1),
            jnp.sum(fresh_rows * fresh_rows, 1),
            jnp.sum(kept_values, 1),
            jnp.sum(kept_values * kept_values, 1),
        ),
        "mp",
    )
    fresh_hat, unused_scale = standardize(fresh_rows, row_stats[0], row_stats[1], full_width)
    kept_hat, kept_inv = standardize(kept_values, row_stats[2], row_stats[3], full_width)
    normed = (fresh_hat * gain_cols + shift_cols).astype(jnp.bfloat16)
    normed_kept = (kept_hat * gain_cols + shift_cols).astype(jnp.bfloat16)
    upstream_all = lax.all_gather(upstream, "mp", axis=0, tiled=True)
    gathered, gathered_kept = (
        lax.all_gather(normed, "dp", axis=0, tiled=True),
        lax.all_gather(normed_kept, "dp", axis=0, tiled=True),
    )
    weight_grad = lax.dot_general(
        gathered_kept, upstream_all, (((0,), (0,)), ((), ())), preferred_element_type=jnp.float32
    )
    segment = gathered
    summed = lax.psum_scatter(
        jnp.dot(segment, weight_tile, preferred_element_type=jnp.float32).astype(jnp.bfloat16),
        "mp",
        scatter_dimension=0,
        tiled=True,
    ).astype(jnp.float32)
    output = (summed + bias.reshape(col_count)).astype(jnp.bfloat16)
    bias_grad = jnp.sum(upstream_all, 0, dtype=jnp.float32)
    segment = upstream_all
    grad_rows = lax.psum_scatter(
        lax.dot_general(
            segment, weight_tile, (((1,), (1,)), ((), ())), preferred_element_type=jnp.float32
        ).astype(jnp.bfloat16),
        "dp",
        scatter_dimension=0,
        tiled=True,
    ).astype(jnp.float32)
    scaled = grad_rows * gain_cols
    column_grads = lax.psum((jnp.sum(grad_rows * kept_hat, 0), jnp.sum(grad_rows, 0)), "dp")
    row_terms = lax.psum((jnp.sum(scaled, 1), jnp.sum(scaled * kept_hat, 1)), "mp")
    input_grad = (
        kept_inv[:, None]
        * (
            scaled
            - row_terms[0][:, None] / full_width
            - kept_hat * (row_terms[1][:, None] / full_width)
        )
    ).astype(jnp.bfloat16)
    out_pack = output.reshape(groups, piece_rows, groups, piece_cols).transpose(0, 2, 1, 3)
    grad_pack = input_grad.reshape(groups, piece_rows, groups, piece_cols).transpose(2, 0, 1, 3)
    outgoing = jnp.where(section_index == 0, out_pack, grad_pack)
    arrived = from_partner(regroup(outgoing, groups), "section", 0)
    as_cotangent = arrived.transpose(0, 2, 1, 3).reshape(row_count, col_count)
    as_input = arrived.transpose(1, 2, 0, 3).reshape(row_count, col_count)
    next_in = jnp.where(section_index == 0, as_cotangent, as_input)
    passed = jnp.where(section_index == 0, input_grad, output)
    return (
        next_in.reshape(fwd_in.shape),
        passed.reshape(fwd_in.shape),
        weight_grad.reshape(1, col_count, col_count),
        bias_grad.reshape(1, col_count),
        jnp.stack([column_grads[0], column_grads[1]]).reshape(1, 2, col_count),
    )


PAIRS = [(0, 1), (1, 0), (2, 3), (3, 2)]
MIDDLE = [(1, 2), (2, 1)]
INWARD = [(0, 1), (3, 2)]
OUTWARD = [(1, 0), (2, 3)]


def shards_of_four(fwd_in, kept_in, cotangent, weight, bias, norm_gain, norm_shift):
    f32, bf16 = jnp.float32, jnp.bfloat16
    section = lax.axis_index("section")
    dp, mp = lax.axis_index("dp"), lax.axis_index("mp")
    inner = (dp == 1) | (dp == 2)
    row_count, col_count = fwd_in.shape[3], fwd_in.shape[4]
    full_width = col_count * 4
    half = col_count // 2
    w = weight.reshape(weight.shape[1], weight.shape[2])
    gain = norm_gain.reshape(col_count)
    shift = norm_shift.reshape(col_count)
    fresh_rows = fwd_in.reshape(row_count, col_count)
    kept_rows = kept_in.reshape(row_count, col_count)
    upstream = cotangent.reshape(row_count, col_count)
    along = lambda value, pairs: lax.ppermute(value, "dp", pairs)
    pick = lambda stack, k: lax.dynamic_index_in_dim(stack, k, 0, keepdims=False)

    seq = lambda *values: lax.optimization_barrier(values)
    either = lambda from_inner, from_outer: jnp.where(inner, from_inner, from_outer)

    c_all = lax.all_gather(upstream, "mp", axis=0, tiled=True)
    u1a, u1b = along(fresh_rows, PAIRS), along(fresh_rows, MIDDLE)
    fresh, kept = fresh_rows.astype(f32), kept_rows.astype(f32)
    sums = jnp.stack(
        [jnp.sum(fresh, 1), jnp.sum(fresh * fresh, 1), jnp.sum(kept, 1), jnp.sum(kept * kept, 1)]
    )
    sums = sums + flip(sums, "mp", 1)
    stats = (sums + flip(sums, "mp", 2)) / full_width
    kept_inv = lax.rsqrt(stats[3] - stats[2] * stats[2] + eps)
    normed_kept = normed(kept_rows, stats[2:], gain, shift)
    pair_stats = jnp.stack([stats[:2], along(stats[:2], PAIRS)])
    u1a, u1b, normed_kept, pair_stats = seq(u1a, u1b, normed_kept, pair_stats)

    a1, b1 = along(either(u1b, normed_kept), PAIRS), along(u1a, MIDDLE)
    h_stack = shares(
        [normed(fresh_rows, stats, gain, shift), normed(u1a, pair_stats[1], gain, shift)],
        w, False, None, 0, 4, 4 * row_count,
    )
    a1, b1, h_stack, c_all, pair_stats = seq(a1, b1, h_stack, c_all, pair_stats)

    a2, b2 = along(b1, OUTWARD), along(a1, MIDDLE)
    all_stats = jnp.concatenate([pair_stats, along(pair_stats, [(s, s ^ 2) for s in range(4)])])
    g_stack = None
    for first in (0, 2):
        blocks = [((c_all, 0, b), (c_all, 1, b)) for b in (first, first + 1)]
        g_stack = shares(blocks, w, True, g_stack, first, 4, 4 * row_count)
    a2, b2, g_stack, all_stats, normed_kept = seq(a2, b2, g_stack, all_stats, normed_kept)
    g_block = lambda k: pick(g_stack, dp ^ k)

    a3, b3 = along(either(b2, g_block(3)), PAIRS), along(normed_kept, MIDDLE)
    two, three = jnp.where(inner, 3, 2), jnp.where(inner, 2, 3)
    h_stack = shares(
        [
            normed(either(u1b, a1), pick(all_stats, two), gain, shift),
            normed(either(b1, a2), pick(all_stats, three), gain, shift),
        ],
        w, False, h_stack, 2, 4, 4 * row_count,
    )
    a3, b3, h_stack = seq(a3, b3, h_stack)

    sent, x2 = turn(g_stack, dp ^ 2, a3, normed_kept, inner)
    h_stack, c_all, x2 = seq(h_stack, c_all, x2)
    a4, b4 = along(sent, PAIRS), along(x2, MIDDLE)
    places = [dp ^ b for b in range(4)]
    places = [jnp.where(inner & (at >= 2), at ^ 1, at) for at in places]
    h_all = reorder(h_stack, places)
    summed = lax.psum_scatter(h_all, "mp", scatter_dimension=0, tiled=True)
    bias_grad = jnp.sum(c_all, 0, dtype=f32)
    c_all = reorder(c_all.reshape(4, row_count, col_count), [dp, dp ^ 1, dp ^ two, dp ^ three])
    a4, b4, c_all, bias_grad = seq(a4, b4, c_all, bias_grad)

    one, two_sums = joint_sums(g_stack, dp ^ 1, dp ^ 3, b4, a4)
    a5, b5 = along(one, PAIRS), along(two_sums, MIDDLE)
    near3 = [along(b3[:, :half], OUTWARD), None]
    a5, b5, near3[0], b3 = seq(a5, b5, near3[0], b3)

    near3[1] = along(b3[:, half:], OUTWARD)
    grad_rows, row_terms, column_sums = gradient(
        g_stack, dp, a5, b5, kept_rows, jnp.stack([stats[2], kept_inv], 1), gain
    )
    row_terms = row_terms.T
    row_terms = row_terms + flip(row_terms, "mp", 1)
    column_sums = column_sums + along(column_sums, PAIRS)
    row_terms, column_sums = seq(row_terms, column_sums)
    row_terms = (row_terms + flip(row_terms, "mp", 2)) / full_width
    column_grads = column_sums + along(column_sums, [(s, s ^ 2) for s in range(4)])
    columns = jnp.stack([stats[2], kept_inv, row_terms[0], row_terms[1]], 1)
    near3[1], columns, column_grads = seq(near3[1], columns, column_grads)
    passed, outgoing = boundary(
        grad_rows, kept_rows, columns, gain, summed, bias.reshape(col_count), section
    )
    arrived = lax.all_to_all(outgoing, ("dp", "mp"), split_axis=0, concat_axis=0, tiled=True)

    c_all, outgoing, near3[0], normed_kept = seq(c_all, outgoing, near3[0], normed_kept)
    early = [normed_kept, either(a1, a4), either(b2, a3)]
    weight_grad = None
    for k in range(2):
        cut = lambda value: value[:, k * half:(k + 1) * half]
        own, one, three = (cut(value) for value in early)
        last = near3[k]
        if weight_grad is not None:
            last, weight_grad = seq(last, weight_grad)
        kept_all = jnp.concatenate([own, one, either(cut(b3), last), three])
        weight_grad = grad_block(kept_all, c_all, weight_grad, k, 2)
    arrived, weight_grad = seq(arrived, weight_grad)
    next_in = joined(flip(arrived, "section", 1), section)

    return (
        next_in.reshape(fwd_in.shape),
        passed.reshape(fwd_in.shape),
        weight_grad.reshape(weight.shape),
        bias_grad.reshape(1, col_count),
        column_grads.reshape(1, 2, col_count),
    )


def shards(*arrays):
    if lax.axis_size("dp") == 4 and lax.axis_size("mp") == 4:
        return shards_of_four(*arrays)
    return shards_of_any_size(*arrays)


def solution(mesh):
    placed = (
        P("section", "dp", "mp", None, None),
        P("section", "dp", "mp", None, None),
        P("section", "dp", "mp", None, None),
        P("section", "mp", "dp"),
        P("section", "dp"),
        P("section", "mp"),
        P("section", "mp"),
    )
    return jax.shard_map(
        shards,
        mesh=mesh,
        in_specs=placed,
        out_specs=(
            P("section", "dp", "mp", None, None),
            P("section", "dp", "mp", None, None),
            P("section", "mp", "dp"),
            P("section", "dp"),
            P("section", None, "mp"),
        ),
        check_vma=False,
    )
```

```python
import functools

import jax
import jax.numpy as jnp
from jax import lax
from jax.experimental import pallas as pl
from jax.experimental.pallas import tpu as pltpu
from jax.sharding import PartitionSpec as P

eps = 1e-05
LIGHT = pl.CostEstimate(flops=1, bytes_accessed=1, transcendentals=0)


def flip(value, axis, mask):
    n = lax.axis_size(axis)
    return lax.ppermute(value, axis, [(s, s ^ mask) for s in range(n)])


def grad_kernel(v_ref, c_ref, *rest):
    out_ref, turned = rest[-2:]

    @pl.when(pl.program_id(0) == 0)
    def _():
        turned[...] = v_ref[...].T

    out_ref[...] = jnp.dot(turned[...], c_ref[...], preferred_element_type=jnp.float32)


def grad_block(kept_block, upstream, filled, block, blocks):
    tokens, width = kept_block.shape
    cols = upstream.shape[1]
    step = 768
    specs = [
        pl.BlockSpec((tokens, width), lambda j: (0, 0)),
        pl.BlockSpec((tokens, step), lambda j: (0, j)),
    ]
    operands = [kept_block, upstream]
    aliases = {}
    if filled is not None:
        specs.append(pl.BlockSpec(memory_space=pl.ANY))
        operands.append(filled)
        aliases = {2: 0}
    return pl.pallas_call(
        grad_kernel,
        grid=(cols // step,),
        in_specs=specs,
        out_specs=pl.BlockSpec((width, step), lambda j: (block, j)),
        out_shape=jax.ShapeDtypeStruct((width * blocks, cols), jnp.float32),
        scratch_shapes=[pltpu.VMEM((width, tokens), jnp.bfloat16)],
        input_output_aliases=aliases,
        compiler_params=pltpu.CompilerParams(vmem_limit_bytes=32 * 2**20),
        cost_estimate=LIGHT,
    )(*operands)


def share_kernel(count, turned, *refs):
    w_ref, out_ref = refs[2 * count], refs[-1]
    half = refs[0].shape[1]
    for k in range(count):
        total = None
        for side in range(2):
            cut = pl.ds(side * half, half)
            part = lax.dot_general(
                refs[2 * k + side][...],
                w_ref[:, cut] if turned else w_ref[cut, :],
                (((1,), (1 if turned else 0,)), ((), ())),
                preferred_element_type=jnp.float32,
            )
            total = part if total is None else total + part
        out_ref[k] = total.astype(jnp.bfloat16)


def shares(blocks, w, turned, filled, at, total):
    count = len(blocks)
    halves = []
    for block in blocks:
        halves += list(block) if isinstance(block, tuple) else [(block, 0), (block, 1)]
    rows = halves[0][0].shape[0]
    depth = w.shape[1] if turned else w.shape[0]
    cols = w.shape[0] if turned else w.shape[1]
    step = 512
    specs = [
        pl.BlockSpec((rows, depth // 2), functools.partial(lambda side, j: (0, side), side))
        for array, side in halves
    ]
    if turned:
        specs.append(pl.BlockSpec((step, depth), lambda j: (j, 0)))
    else:
        specs.append(pl.BlockSpec((depth, step), lambda j: (0, j)))
    operands = [array for array, side in halves] + [w]
    aliases = {}
    if filled is not None:
        specs.append(pl.BlockSpec(memory_space=pl.ANY))
        operands.append(filled)
        aliases = {2 * count + 1: 0}
    return pl.pallas_call(
        functools.partial(share_kernel, count, turned),
        grid=(cols // step,),
        in_specs=specs,
        out_specs=pl.BlockSpec((count, rows, step), lambda j: (at // count, 0, j)),
        out_shape=jax.ShapeDtypeStruct((total, rows, cols), jnp.bfloat16),
        input_output_aliases=aliases,
        compiler_params=pltpu.CompilerParams(vmem_limit_bytes=32 * 2**20),
        cost_estimate=LIGHT,
    )(*operands)


def boundary_kernel(upper_ref, lower_ref, kept_ref, columns_ref, gain_ref, h_ref, bias_ref, section_ref, passed_ref, out_ref):
    step = pl.program_id(0)
    first = section_ref[0] == 0
    groups = pl.num_programs(0)
    width = out_ref.shape[2]
    f32 = jnp.float32
    columns = columns_ref[...]
    mean, inverse, one, two = (columns[:, k:k + 1] for k in range(4))
    for f in range(out_ref.shape[0] // 4):
        cut = pl.ds(f * width, width)
        hat = (kept_ref[:, cut].astype(f32) - mean) * inverse
        rows = jnp.where(step < 2, upper_ref[:, cut], lower_ref[:, cut])
        grad = (inverse * (rows * gain_ref[:, cut] - one - hat * two)).astype(jnp.bfloat16)
        output = (h_ref[:, cut].astype(f32) + bias_ref[:, cut]).astype(jnp.bfloat16)
        passed_ref[:, cut] = jnp.where(first, grad, output)
        out_ref[jnp.where(first, step * groups + f, f * groups + step)] = jnp.where(
            first, output, grad
        )


def boundary(upper, lower, kept_rows, columns, gain, summed, bias, section):
    rows, cols = kept_rows.shape
    part = rows // 4
    wide = pl.BlockSpec((part, cols), lambda j: (j, 0))
    line = pl.BlockSpec((1, cols), lambda j: (0, 0))
    return pl.pallas_call(
        boundary_kernel,
        grid=(4,),
        in_specs=[
            pl.BlockSpec((part, cols), lambda j: (jnp.minimum(j, 1), 0)),
            pl.BlockSpec((part, cols), lambda j: (jnp.maximum(j - 2, 0), 0)),
            wide, pl.BlockSpec((part, 4), lambda j: (j, 0)), line, wide, line,
            pl.BlockSpec(memory_space=pltpu.SMEM),
        ],
        out_specs=[wide, pl.BlockSpec((16, part, cols // 4), lambda j: (0, 0, 0))],
        out_shape=[
            jax.ShapeDtypeStruct((rows, cols), jnp.bfloat16),
            jax.ShapeDtypeStruct((16, part, cols // 4), jnp.bfloat16),
        ],
        compiler_params=pltpu.CompilerParams(vmem_limit_bytes=32 * 2**20),
        cost_estimate=LIGHT,
    )(
        upper, lower, kept_rows, columns, gain.reshape(1, cols), summed, bias.reshape(1, cols),
        section.reshape(1),
    )


def joined_kernel(pieces_ref, section_ref, out_ref):
    step = pl.program_id(0)
    width = pieces_ref.shape[2]
    for c in range(4):
        piece = jnp.where(section_ref[0] == 0, step * 4 + c, c * 4 + step)
        out_ref[:, pl.ds(c * width, width)] = pieces_ref[piece]


def joined(pieces, section):
    count, part, width = pieces.shape
    return pl.pallas_call(
        joined_kernel,
        grid=(4,),
        in_specs=[
            pl.BlockSpec((count, part, width), lambda j: (0, 0, 0)),
            pl.BlockSpec(memory_space=pltpu.SMEM),
        ],
        out_specs=pl.BlockSpec((part, 4 * width), lambda j: (j, 0)),
        out_shape=jax.ShapeDtypeStruct((4 * part, 4 * width), pieces.dtype),
        compiler_params=pltpu.CompilerParams(vmem_limit_bytes=32 * 2**20),
        cost_estimate=LIGHT,
    )(pieces, section.reshape(1))


def from_partner(value, axis, stride):
    mask = 2**stride
    pairs = [(source, source ^ mask) for source in range(lax.axis_size(axis))]
    return lax.ppermute(value, axis, pairs)


def standardize(values, totals, squares, full_width):
    mean_val = totals / full_width
    spread = squares / full_width - mean_val * mean_val
    inv_std = lax.rsqrt(spread + eps)
    return ((values - mean_val[:, None]) * inv_std[:, None], inv_std)


def regroup(outgoing, groups):
    flat_buffer = outgoing.reshape((groups * groups,) + outgoing.shape[2:])
    moved_data = lax.all_to_all(flat_buffer, ("dp", "mp"), split_axis=0, concat_axis=0, tiled=True)
    return moved_data.reshape(outgoing.shape)


def shards_of_any_size(fwd_in, kept_in, cotangent, weight, bias, norm_gain, norm_shift):
    section_index = lax.axis_index("section")
    groups = lax.axis_size("dp")
    row_count = fwd_in.shape[3]
    col_count = fwd_in.shape[4]
    full_width = col_count * lax.axis_size("mp")
    piece_rows = row_count // groups
    piece_cols = col_count // groups
    weight_tile = weight.reshape(col_count, col_count)
    gain_cols = norm_gain.reshape(col_count)
    shift_cols = norm_shift.reshape(col_count)
    fresh_rows = fwd_in.reshape(row_count, col_count).astype(jnp.float32)
    kept_values = kept_in.reshape(row_count, col_count).astype(jnp.float32)
    upstream = cotangent.reshape(row_count, col_count)
    row_stats = lax.psum(
        (
            jnp.sum(fresh_rows, 1),
            jnp.sum(fresh_rows * fresh_rows, 1),
            jnp.sum(kept_values, 1),
            jnp.sum(kept_values * kept_values, 1),
        ),
        "mp",
    )
    fresh_hat, unused_scale = standardize(fresh_rows, row_stats[0], row_stats[1], full_width)
    kept_hat, kept_inv = standardize(kept_values, row_stats[2], row_stats[3], full_width)
    normed = (fresh_hat * gain_cols + shift_cols).astype(jnp.bfloat16)
    normed_kept = (kept_hat * gain_cols + shift_cols).astype(jnp.bfloat16)
    upstream_all = lax.all_gather(upstream, "mp", axis=0, tiled=True)
    gathered, gathered_kept = (
        lax.all_gather(normed, "dp", axis=0, tiled=True),
        lax.all_gather(normed_kept, "dp", axis=0, tiled=True),
    )
    weight_grad = lax.dot_general(
        gathered_kept, upstream_all, (((0,), (0,)), ((), ())), preferred_element_type=jnp.float32
    )
    segment = gathered
    summed = lax.psum_scatter(
        jnp.dot(segment, weight_tile, preferred_element_type=jnp.float32).astype(jnp.bfloat16),
        "mp",
        scatter_dimension=0,
        tiled=True,
    ).astype(jnp.float32)
    output = (summed + bias.reshape(col_count)).astype(jnp.bfloat16)
    bias_grad = jnp.sum(upstream_all, 0, dtype=jnp.float32)
    segment = upstream_all
    grad_rows = lax.psum_scatter(
        lax.dot_general(
            segment, weight_tile, (((1,), (1,)), ((), ())), preferred_element_type=jnp.float32
        ).astype(jnp.bfloat16),
        "dp",
        scatter_dimension=0,
        tiled=True,
    ).astype(jnp.float32)
    scaled = grad_rows * gain_cols
    column_grads = lax.psum((jnp.sum(grad_rows * kept_hat, 0), jnp.sum(grad_rows, 0)), "dp")
    row_terms = lax.psum((jnp.sum(scaled, 1), jnp.sum(scaled * kept_hat, 1)), "mp")
    input_grad = (
        kept_inv[:, None]
        * (
            scaled
            - row_terms[0][:, None] / full_width
            - kept_hat * (row_terms[1][:, None] / full_width)
        )
    ).astype(jnp.bfloat16)
    out_pack = output.reshape(groups, piece_rows, groups, piece_cols).transpose(0, 2, 1, 3)
    grad_pack = input_grad.reshape(groups, piece_rows, groups, piece_cols).transpose(2, 0, 1, 3)
    outgoing = jnp.where(section_index == 0, out_pack, grad_pack)
    arrived = from_partner(regroup(outgoing, groups), "section", 0)
    as_cotangent = arrived.transpose(0, 2, 1, 3).reshape(row_count, col_count)
    as_input = arrived.transpose(1, 2, 0, 3).reshape(row_count, col_count)
    next_in = jnp.where(section_index == 0, as_cotangent, as_input)
    passed = jnp.where(section_index == 0, input_grad, output)
    return (
        next_in.reshape(fwd_in.shape),
        passed.reshape(fwd_in.shape),
        weight_grad.reshape(1, col_count, col_count),
        bias_grad.reshape(1, col_count),
        jnp.stack([column_grads[0], column_grads[1]]).reshape(1, 2, col_count),
    )


PAIRS = [(0, 1), (1, 0), (2, 3), (3, 2)]
MIDDLE = [(1, 2), (2, 1)]
INWARD = [(0, 1), (3, 2)]
OUTWARD = [(1, 0), (2, 3)]


def shards_of_four(fwd_in, kept_in, cotangent, weight, bias, norm_gain, norm_shift):
    f32, bf16 = jnp.float32, jnp.bfloat16
    section = lax.axis_index("section")
    dp, mp = lax.axis_index("dp"), lax.axis_index("mp")
    inner = (dp == 1) | (dp == 2)
    row_count, col_count = fwd_in.shape[3], fwd_in.shape[4]
    full_width = col_count * 4
    half = col_count // 2
    w = weight.reshape(weight.shape[1], weight.shape[2])
    gain = norm_gain.reshape(col_count)
    shift = norm_shift.reshape(col_count)
    fresh_rows = fwd_in.reshape(row_count, col_count)
    kept_rows = kept_in.reshape(row_count, col_count)
    upstream = cotangent.reshape(row_count, col_count)
    along = lambda value, pairs: lax.ppermute(value, "dp", pairs)
    pick = lambda stack, k: lax.dynamic_index_in_dim(stack, k, 0, keepdims=False)

    def standardize(values, mean, square_mean):
        inverse = lax.rsqrt(square_mean - mean * mean + eps)
        return (values.astype(f32) - mean[:, None]) * inverse[:, None], inverse

    def affine(hat):
        return (hat * gain + shift).astype(bf16)

    def added(one, two):
        return (one.astype(f32) + two.astype(f32)).astype(bf16)

    seq = lambda *values: lax.optimization_barrier(values)

    u1a, u1b = along(fresh_rows, PAIRS), along(fresh_rows, MIDDLE)
    c_left, c_right = upstream[:, :half], upstream[:, half:]
    c1_left, c2_right = flip(c_left, "mp", 1), flip(c_right, "mp", 2)
    fresh, kept = fresh_rows.astype(f32), kept_rows.astype(f32)
    sums = jnp.stack(
        [jnp.sum(fresh, 1), jnp.sum(fresh * fresh, 1), jnp.sum(kept, 1), jnp.sum(kept * kept, 1)]
    )
    other = flip(sums, "mp", 1)
    g_stack = shares([upstream], w, True, None, 3, 4)
    c1_left, c2_right, sums, other, g_stack = seq(c1_left, c2_right, sums, other, g_stack)
    c_from_one = flip(jnp.concatenate([c_right, c2_right], 1), "mp", 1)
    c_from_two = flip(jnp.concatenate([c_left, c1_left], 1), "mp", 2)
    sums = sums + other
    stats = (sums + flip(sums, "mp", 2)) / full_width
    kept_hat, kept_inv = standardize(kept_rows, stats[2], stats[3])
    normed_kept = affine(kept_hat)

    def normed(rows, row_stats):
        hat, unused = standardize(rows, row_stats[0], row_stats[1])
        return affine(hat)

    pair_stats = jnp.stack([stats[:2], along(stats[:2], PAIRS)])
    h_stack = shares([normed(fresh_rows, stats)], w, False, None, 0, 4)
    u1a, u1b, normed_kept, h_stack = seq(u1a, u1b, normed_kept, h_stack)

    sides = [slice(0, row_count // 2), slice(row_count // 2, row_count)]
    either = lambda from_inner, from_outer: jnp.where(inner, from_inner, from_outer)
    a1, b1, a2, b2, a3, b3, a4, b4, a5, b5, x2 = ([None, None] for unused in range(11))

    for k in range(2):
        a1[k] = along(either(u1b[sides[k]], normed_kept[sides[k]]), PAIRS)
        b1[k] = along(u1a[sides[k]], MIDDLE)
    h_stack = shares([normed(u1a, pair_stats[1])], w, False, h_stack, 1, 4)

    a1[0], b1[0], h_stack, c1_left, c2_right = seq(a1[0], b1[0], h_stack, c1_left, c2_right)
    a2[0], b2[0] = along(b1[0], OUTWARD), along(a1[0], MIDDLE)
    g_stack = shares(
        [((c1_left, 0), (c_from_one, 0)), ((c_from_two, 0), (c2_right, 0))], w, True, g_stack, 0, 4
    )
    a1[1], b1[1], g_stack = seq(a1[1], b1[1], g_stack)
    a2[1], b2[1] = along(b1[1], OUTWARD), along(a1[1], MIDDLE)
    pair_stats = seq(pair_stats, b1[1])[0]
    all_stats = jnp.concatenate([pair_stats, along(pair_stats, [(s, s ^ 2) for s in range(4)])])
    g_stack = shares([((c_from_two, 1), (c_from_one, 1))], w, True, g_stack, 2, 4)

    def g_block(k, side):
        apart = lax.bitwise_xor(lax.bitwise_xor(dp, mp), k)
        at = jnp.where(apart == 0, 3, apart - 1)
        return lax.dynamic_slice(
            g_stack, (at, side.start, 0), (1, side.stop - side.start, col_count)
        )[0]

    a2[0], b2[0], g_stack, normed_kept = seq(a2[0], b2[0], g_stack, normed_kept)
    sent, h_stack = seq(either(b2[0], g_block(3, sides[0])), h_stack)
    a3[0] = along(sent, PAIRS)
    b3[0] = along(normed_kept[sides[0]], MIDDLE)
    all_stats, h_stack = seq(all_stats, h_stack)
    u2 = jnp.where(inner, u1b, jnp.concatenate(a1))
    h_stack = shares([normed(u2, pick(all_stats, jnp.where(inner, 3, 2)))], w, False, h_stack, 2, 4)
    a2[1], b2[1], h_stack, normed_kept = seq(a2[1], b2[1], h_stack, normed_kept)
    sent, h_stack = seq(either(b2[1], g_block(3, sides[1])), h_stack)
    a3[1] = along(sent, PAIRS)
    b3[1] = along(normed_kept[sides[1]], MIDDLE)
    u3 = jnp.where(inner, jnp.concatenate(b1), jnp.concatenate(a2))
    h_stack = shares([normed(u3, pick(all_stats, jnp.where(inner, 2, 3)))], w, False, h_stack, 3, 4)

    nothing = jnp.zeros((row_count // 2, col_count), bf16)

    def fourth(k, chain):
        x2[k] = added(g_block(2, sides[k]), jnp.where(inner, a3[k], nothing))
        sent, x2[k], chain = seq(either(normed_kept[sides[k]], x2[k]), x2[k], chain)
        a4[k], b4[k] = along(sent, PAIRS), along(x2[k], MIDDLE)
        return chain

    a3[0], b3[0], h_stack = seq(a3[0], b3[0], h_stack)
    h_stack = fourth(0, h_stack)

    def h_block(b):
        apart = lax.bitwise_xor(dp, b)
        return pick(h_stack, jnp.where(inner & (apart >= 2), apart ^ 1, apart))

    h_all = jnp.concatenate([h_block(b) for b in range(4)])
    a3[1], b3[1], h_all = seq(a3[1], b3[1], h_all)
    summed = lax.psum_scatter(h_all, "mp", scatter_dimension=0, tiled=True)
    own_block = fourth(1, upstream)
    c_stack = jnp.stack(
        [
            own_block,
            jnp.concatenate([c1_left, c_from_one[:, :half]], 1),
            jnp.concatenate([c_from_two[:, :half], c2_right], 1),
            jnp.concatenate([c_from_two[:, half:], c_from_one[:, half:]], 1),
        ]
    )
    block_sums = jnp.sum(c_stack, 1, dtype=f32)
    in_order = [pick(block_sums, lax.bitwise_xor(mp, b)) for b in range(4)]
    bias_grad = in_order[0] + in_order[1] + in_order[2] + in_order[3]
    c_of = lambda k: pick(c_stack, lax.bitwise_xor(lax.bitwise_xor(dp, mp), k))
    c_all = jnp.concatenate(
        [c_of(0), c_of(1), c_of(jnp.where(inner, 3, 2)), c_of(jnp.where(inner, 2, 3))]
    )

    def fifth(k, chain):
        one, two, chain = seq(
            added(g_block(1, sides[k]), b4[k]), added(g_block(3, sides[k]), a4[k]), chain
        )
        a5[k], b5[k] = along(one, PAIRS), along(two, MIDDLE)
        return chain

    a4[0], b4[0], c_all = seq(a4[0], b4[0], c_all)
    c_all = fifth(0, c_all)
    a4[1], b4[1], c_all = seq(a4[1], b4[1], c_all)
    c_all = fifth(1, c_all)

    def gradient(k):
        rows = g_block(0, sides[k]).astype(f32) + a5[k].astype(f32) + b5[k].astype(f32)
        scaled, hat = rows * gain, kept_hat[sides[k]]
        return (
            rows,
            jnp.stack([jnp.sum(scaled, 1), jnp.sum(scaled * hat, 1)]),
            jnp.stack([jnp.sum(rows * hat, 0), jnp.sum(rows, 0)]),
        )

    near1 = jnp.concatenate(b3)
    a5[0], b5[0], near1, c_all = seq(a5[0], b5[0], near1, c_all)
    near3 = [along(near1[:, :half], OUTWARD), along(near1[:, half:], OUTWARD)]
    upper, upper_terms, upper_sums = gradient(0)
    a5[1], b5[1], upper_terms, upper_sums = seq(a5[1], b5[1], upper_terms, upper_sums)
    lower, lower_terms, lower_sums = gradient(1)
    row_terms = jnp.concatenate([upper_terms, lower_terms], 1)
    row_terms = row_terms + flip(row_terms, "mp", 1)
    row_terms = (row_terms + flip(row_terms, "mp", 2)) / full_width
    columns = jnp.stack([stats[2], kept_inv, row_terms[0], row_terms[1]], 1)
    near3[0], near3[1], columns = seq(near3[0], near3[1], columns)
    passed, outgoing = boundary(
        upper, lower, kept_rows, columns, gain, summed, bias.reshape(col_count), section
    )
    arrived = lax.all_to_all(outgoing, ("dp", "mp"), split_axis=0, concat_axis=0, tiled=True)

    column_sums, c_all, outgoing = seq(upper_sums + lower_sums, c_all, outgoing)
    column_sums = column_sums + along(column_sums, PAIRS)
    column_grads = column_sums + along(column_sums, [(s, s ^ 2) for s in range(4)])
    width = half // 2
    early = [
        normed_kept,
        jnp.where(inner, jnp.concatenate(a1), jnp.concatenate(a4)),
        jnp.where(inner, jnp.concatenate(b2), jnp.concatenate(a3)),
    ]
    weight_grad = None
    for k in range(4):
        last = near3[k // 2]
        if weight_grad is None:
            last, c_all = seq(last, c_all)
        else:
            last, weight_grad = seq(last, weight_grad)
        cut = lambda value: value[:, k * width:(k + 1) * width]
        own, one, three = (cut(value) for value in early)
        two = jnp.where(inner, cut(near1), last[:, (k % 2) * width:(k % 2 + 1) * width])
        weight_grad = grad_block(
            jnp.concatenate([own, one, two, three]), c_all, weight_grad, k, 4
        )
        if k == 2:
            arrived, column_grads, weight_grad = seq(arrived, column_grads, weight_grad)
            arrived = flip(arrived, "section", 1)
    next_in = joined(arrived, section)

    return (
        next_in.reshape(fwd_in.shape),
        passed.reshape(fwd_in.shape),
        weight_grad.reshape(weight.shape),
        bias_grad.reshape(1, col_count),
        column_grads.reshape(1, 2, col_count),
    )


def shards(*arrays):
    if lax.axis_size("dp") == 4 and lax.axis_size("mp") == 4:
        return shards_of_four(*arrays)
    return shards_of_any_size(*arrays)


def solution(mesh):
    placed = (
        P("section", "dp", "mp", None, None),
        P("section", "dp", "mp", None, None),
        P("section", "dp", "mp", None, None),
        P("section", "mp", "dp"),
        P("section", "dp"),
        P("section", "mp"),
        P("section", "mp"),
    )
    return jax.shard_map(
        shards,
        mesh=mesh,
        in_specs=placed,
        out_specs=(
            P("section", "dp", "mp", None, None),
            P("section", "dp", "mp", None, None),
            P("section", "mp", "dp"),
            P("section", "dp"),
            P("section", None, "mp"),
        ),
        check_vma=False,
    )
```
